256 devices in a mesh: comp: 4 (over z_hi), lat: 4 (over x), lon: 16 (over z_lo, y, core).
Axes of the slice: x: 4, y: 4, z: 8 (z_hi: 4, z_lo: 2; z = z_hi * 2 + z_lo), core: 2. Of those that a mesh axis runs over, the one named last changes fastest.
Arguments:
- checkpoint: float32 [4, 6, 2, 256, 4096], P('comp', None, None, 'lat', 'lon'), may hold values from -6 to 6
- adjoint_in: float32 [4, 6, 2, 256, 4096], P('comp', None, None, 'lat', 'lon'), may hold values from -6 to 6
- land_mask: int32 [256, 4096], P('lat', 'lon'), may hold values 0 or 1
- diffusivity: float32 [6], replicated, may hold values from 0.02 to 0.2
- penetration: float32 [6], replicated, may hold values from 0.2 to 1
- column_weight: float32 [4, 192], replicated, may hold values from -0.4375 to 0.4375
- routes: int32 [16384, 1], P(('lat', 'lon')), may hold values from 0 to 63; in each aligned block of 256 rows (0 to 255, 256 to 511, ...) at most 8 rows name the same one
- dest_row: int32 [16384], P(('lat', 'lon')), may hold values from 0 to 63
- weight_id: int32 [16384], P(('lat', 'lon')), may hold values from 0 to 7
- regrid_table: float32 [8, 4], replicated, may hold values from 0.25 to 1
Outputs:
- adjoint_out: float32 [4, 6, 2, 256, 4096], P('comp', None, None, 'lat', 'lon')
The draws below stay inside these ranges and needn't reach their ends.
Inputs may be any that keep to these rules, and one draw needn't show every extreme that they name: `routes`: among the rows of one atmosphere tile no ocean tile is named more than 8 times, a bound that some block reaches.
All inputs are finite; a program needn't handle non-finite values. No bound on the sum of `land_mask` on one device may be relied on, other than what follows from the above.
Results may differ from the reference program's by a relative error of at most 0.00011.
Values sent between devices are 32-bit elements; how exact they have to be, the bound alone decides.
No kernel may reach another device: no remote copies, remote signals or barrier semaphores. Data moves between devices by JAX's collectives and lax.ppermute only.
A program may use at most 64 MiB of HBM per device.

```python
import math
import jax
import jax.numpy as jnp
import numpy as np
from jax import lax

FLD = 6
NFLUX = 4
LEVB = 2
NSTEP = 4
NW = 8
CLAT = 64
CLON = 256
ALEV = 32
ACOLS = 1024
AROWS = 256
TILES = 64
MOST = 8
ALLROWS = 16384
NLAT = 256
NLON = 4096
SECTIONS = 4
OLEV = 6
N_COMP = 4
N_LAT = 4
N_LON = 16


def touch_ends(drawn, rng, smallest, largest):
    index_at = [jax.random.randint(jax.random.fold_in(rng, axis), (), 0, length) for axis, length in enumerate(drawn.shape)]
    longest = drawn.shape.index(max(drawn.shape))
    next_to = index_at[:longest] + [(index_at[longest] + 1) % drawn.shape[longest]] + index_at[longest + 1:]
    return drawn.at[tuple(index_at)].set(smallest).at[tuple(next_to)].set(largest)


def steps_of(key, extent, cuts, smallest, high):
    level, own = 1.0, jax.random.fold_in(key, 6)
    for dim, parts in cuts:
        heights = jnp.exp(jax.random.uniform(jax.random.fold_in(own, dim), (parts,), jnp.float32, smallest / len(cuts), high / len(cuts)))
        level = level * jnp.repeat(heights, extent[dim] // parts).reshape([-1 if axis == dim else 1 for axis in range(len(extent))])
    return level


def routed_block(key, own, number, rows, count, top, bound, skew):
    ranking = jax.random.permutation(key, count)
    packed, ordinary = portions_of(count, rows * top, bound, skew, True), portions_of(count, rows * top, bound, skew, False)
    places = jnp.arange(count)

    def named(lengths, turn):
        used = int((lengths > 0).sum())
        fixed = max(1, used // 4)
        shifted = fixed + (places - fixed + turn * (used - fixed)) % max(1, count - fixed)
        return jnp.zeros((count,), jnp.int32).at[ranking[jnp.where(places < fixed, places, shifted)]].set(jnp.asarray(lengths, jnp.int32))

    lengths = jnp.where(number % 4 == 0, named(packed, number // 4), named(ordinary, number - number // 4 - 1))
    mixed = jax.random.permutation(jax.random.fold_in(own, 3), count)
    donor, taker = mixed[0:count // 2 * 2:2], mixed[1:count // 2 * 2:2]
    margin = jnp.minimum(lengths[donor] - 1, bound - lengths[taker]) // 2
    margin = jnp.where((donor == ranking[0]) | (taker == ranking[0]) | (lengths[taker] == 0), 0, jnp.maximum(margin, 0))
    shifted = jax.random.randint(jax.random.fold_in(own, 4), (count // 2,), 0, 1 << 20) % (margin + 1)
    lengths = lengths.at[donor].add(-shifted).at[taker].add(shifted)
    items = jnp.searchsorted(jnp.cumsum(lengths), jnp.arange(rows * top), side="right").astype(jnp.int32)
    listing = items.reshape(top, rows).T
    listing = listing[jax.random.permutation(jax.random.fold_in(own, 1), rows)]
    turn = jax.random.randint(jax.random.fold_in(own, 2), (rows, 1), 0, top)
    return jnp.take_along_axis(listing, (jnp.arange(top)[None, :] + turn) % top, axis=1)


def portions_of(count, total, reach, lean, full):
    weights = [(1 << 20) // math.isqrt(standing ** lean) + 1 for standing in range(1, count + 1)]
    largest = reach if full else min(reach, max(-(-total // count), total * weights[0] // sum(weights)))
    least = 1 if total - largest >= count - 1 else 0
    counts, spare = [largest] + [least] * (count - 1), total - largest - least * (count - 1)
    while spare > 0:
        free = [i for i in range(1, count) if counts[i] < largest] or [i for i in range(1, count) if counts[i] < reach]
        pool, budget = sum([weights[i] for i in free]), spare
        for i in free:
            more = min(reach - counts[i], max(1, budget * weights[i] // pool), spare)
            counts[i] = counts[i] + more
            spare = spare - more
    return np.array(counts)


def gaussian(own_key, shape, deviation, bound, shards=(), dtype=jnp.bfloat16):
    result = deviation * jax.random.normal(own_key, shape, jnp.float32)
    if shards:
        result = result * steps_of(own_key, shape, shards, -0.22, 0.18)
    return jnp.clip(result, -bound, bound).astype(dtype)


def setup_inputs(seed: int = 0) -> dict:
    splits = jax.random.split(jax.random.key(seed), 11)
    checkpoint = gaussian(splits[0], (SECTIONS, FLD, LEVB, NLAT, NLON), 1.0, 6.0, ((0, 4), (3, 4), (4, 16)), jnp.float32)
    adjoint_in = gaussian(splits[1], (SECTIONS, FLD, LEVB, NLAT, NLON), 1.0, 6.0, ((0, 4), (3, 4), (4, 16)), jnp.float32)
    land_mask = touch_ends((jax.random.randint(splits[2], (NLAT, NLON), 0, 4) < 3).astype(jnp.int32), jax.random.fold_in(splits[2], 1), 0, 1)
    diffusivity = jnp.clip(jnp.exp(jax.random.uniform(splits[3], (FLD,), jnp.float32, math.log(0.02), math.log(0.2))), 0.02, 0.2)
    penetration = jnp.clip(jnp.exp(jax.random.uniform(splits[4], (OLEV,), jnp.float32, math.log(0.2), math.log(1.0))), 0.2, 1.0)
    column_weight = gaussian(splits[5], (NFLUX, FLD * ALEV), (FLD * ALEV) ** -0.5, 0.4375, (), jnp.float32)
    routes_keys = jax.random.split(jax.random.fold_in(splits[6], 1), ALLROWS // AROWS)
    routes_turns = jax.random.permutation(jax.random.fold_in(splits[6], 3), ALLROWS // AROWS)
    routes = jax.vmap(lambda own, number: routed_block(jax.random.fold_in(splits[6], 2), own, number, AROWS, TILES, 1, MOST, 2))(routes_keys, routes_turns).reshape((ALLROWS, 1))
    dest_row = touch_ends(jax.random.randint(splits[7], (ALLROWS,), 0, CLAT), jax.random.fold_in(splits[7], 1), 0, CLAT - 1).astype(jnp.int32)
    weight_id = touch_ends(jax.random.randint(splits[8], (ALLROWS,), 0, NW), jax.random.fold_in(splits[8], 1), 0, NW - 1).astype(jnp.int32)
    regrid_table = jnp.clip(jnp.exp(jax.random.uniform(splits[9], (NW, 4), jnp.float32, math.log(0.25), math.log(1.0))), 0.25, 1.0)
    return {"checkpoint": checkpoint, "adjoint_in": adjoint_in, "land_mask": land_mask, "diffusivity": diffusivity, "penetration": penetration, "column_weight": column_weight, "routes": routes, "dest_row": dest_row, "weight_id": weight_id, "regrid_table": regrid_table}


SPEED_BASE = 0.5
SPEED_GAIN = 0.5
STEP_COEF = 0.2
exact_mode = lax.Precision.HIGHEST

def advance(padded, diffusivity, wet_mask):
    centre = padded[..., 1:-1, 1:-1]
    east_cell = padded[..., 1:-1, 2:]
    west_cell = padded[..., 1:-1, :-2]
    north_cell = padded[..., 2:, 1:-1]
    south_cell = padded[..., :-2, 1:-1]
    speed_east = SPEED_BASE + SPEED_GAIN * centre[..., 0:1, :, :, :]
    speed_north = SPEED_GAIN * centre[..., 1:2, :, :, :]
    carried = speed_east * (east_cell - west_cell) * 0.5 + speed_north * (north_cell - south_cell) * 0.5
    spread = east_cell + west_cell + north_cell + south_cell - 4.0 * centre
    return wet_mask * (centre - STEP_COEF * carried + diffusivity[:, None, None, None] * spread)

def extend(field):
    wrapped = jnp.concatenate([field[..., -1:], field, field[..., :1]], axis=-1)
    zero_row = jnp.zeros_like(wrapped[..., :1, :])
    return jnp.concatenate([zero_row, wrapped, zero_row], axis=-2)

def reference(checkpoint, adjoint_in, land_mask, diffusivity, penetration, column_weight, routes, dest_row, weight_id, regrid_table):
    band_count = N_COMP - 1
    tile_count = N_LAT * N_LON
    wet_mask = land_mask.astype(jnp.float32)

    def step_field(field):
        return advance(extend(field), diffusivity, wet_mask)
    ocean_state = checkpoint[:band_count]
    saved = []
    for index_step in range(NSTEP):
        saved.append(ocean_state)
        if index_step + 1 < NSTEP:
            ocean_state = step_field(ocean_state)
    sensitivity = adjoint_in[band_count] * (1.0 - jnp.square(jnp.tanh(checkpoint[band_count])))
    tiled = sensitivity.reshape(FLD, LEVB, N_LAT, CLAT, N_LON, CLON).transpose(2, 4, 0, 1, 3, 5).reshape(tile_count, FLD * ALEV, ACOLS)
    surface_flux = jnp.einsum('kc,tca->tka', column_weight, tiled, precision=exact_mode)
    by_segment = surface_flux.reshape(tile_count, NFLUX, CLAT // 4, CLON // 4)
    by_row = jnp.repeat(by_segment, 16, axis=2).transpose(0, 2, 1, 3).reshape(tile_count * AROWS, NFLUX, CLON // 4)
    profile = regrid_table[weight_id]
    values = (by_row[..., None] * profile[:, None, None, :]).reshape(tile_count * AROWS, NFLUX, CLON)
    target = routes[:, 0] * CLAT + dest_row
    summed = jax.ops.segment_sum(values, target, num_segments=tile_count * CLAT)
    forcing = summed.reshape(N_LAT, N_LON, CLAT, NFLUX, CLON).transpose(3, 0, 2, 1, 4).reshape(NFLUX, NLAT, NLON)
    pen_band = penetration.reshape(band_count, LEVB)
    forcing_term = pen_band[:, None, :, None, None] * (wet_mask[None, None] * forcing[:, None])[None]
    spare_fields = jnp.zeros((band_count, FLD - NFLUX, LEVB, NLAT, NLON), jnp.float32)
    adjoint = adjoint_in[:band_count] + jnp.concatenate([forcing_term, spare_fields], axis=1)
    for index_step in reversed(range(NSTEP)):
        pull_back = jax.vjp(step_field, saved[index_step])[1]
        adjoint = pull_back(adjoint)[0]
    return jnp.concatenate([adjoint, sensitivity[None]], axis=0)
```

```python
import jax
import jax.numpy as jnp
from jax import lax
from jax.experimental import pallas as pl
from jax.experimental.pallas import tpu as pltpu
from jax.sharding import PartitionSpec as P

NSTEP = 4
STEP_COEF = 0.2
SPEED_BASE = 0.5
SPEED_GAIN = 0.5

FLD = 6
NFLUX = 4
LEVB = 2
ROWS = 64
COLS = 256
PLANES = FLD * LEVB
HALO_ROWS = 80
ADJ_ROWS = 72
WIDE = 384
LANES = 128
TILES = 64
SEGS = 16
FAR = -1.0

f32 = jnp.float32
bf16 = jnp.bfloat16
VM = pltpu.VMEM
SM = pltpu.SMEM


def vmem():
    return pl.BlockSpec(memory_space=VM)


def smem():
    return pl.BlockSpec(memory_space=SM)


def in_vmem(shape, dtype=f32):
    return VM(shape, dtype)


def east(x):
    return pltpu.roll(x, WIDE - 1, 1)


def west(x):
    return pltpu.roll(x, 1, 1)


def north(x):
    return pltpu.roll(x, x.shape[0] - 1, 0)


def south(x):
    return pltpu.roll(x, 1, 0)


def iota(shape, dim):
    return lax.broadcasted_iota(jnp.int32, shape, dim)


def split(x):
    high = x.astype(bf16)
    return high, (x - high.astype(f32)).astype(bf16)


def dot(x, y):
    return jnp.dot(x, y, preferred_element_type=f32)


def flux_kernel(place, checkpoint, adjoint_in, mask, weight, flux, to_north, to_south):
    for plane in range(PLANES):
        f, l = plane // LEVB, plane % LEVB
        to_north[plane] = checkpoint[f, l, ROWS - 8 : ROWS, :]
        to_south[plane] = checkpoint[f, l, 0:8, :]
        to_north[PLANES + plane] = adjoint_in[f, l, ROWS - 8 : ROWS, :]
        to_south[PLANES + plane] = adjoint_in[f, l, 0:8, :]
    to_north[2 * PLANES] = mask[ROWS - 8 : ROWS, :].astype(f32)
    to_south[2 * PLANES] = mask[0:8, :].astype(f32)

    @pl.when(place[0] == 3)
    def _():
        t = jnp.tanh(checkpoint[...])
        sens = (adjoint_in[...] * (1.0 - t * t)).reshape(PLANES * ROWS, COLS)
        by_kind = jnp.dot(weight[...], sens, precision=lax.Precision.HIGHEST, preferred_element_type=f32)
        rows = []
        for q in range(4):
            rows.append(
                jnp.concatenate(
                    [by_kind[k * 4 : k * 4 + 4, q * 64 : q * 64 + 64] for k in range(NFLUX)], axis=1
                )
            )
        by_seg = jnp.concatenate(rows, axis=0)
        flux[0:16, :] = by_seg[:, 0:LANES]
        flux[16:32, :] = by_seg[:, LANES:]

    @pl.when(place[0] != 3)
    def _():
        flux[...] = jnp.zeros((32, LANES), f32)


def strip_kernel(checkpoint, adjoint_in, mask, from_south, from_north, to_east, to_west):
    lane_group = iota((HALO_ROWS, LANES), 1) // 8
    for kind, source in enumerate((checkpoint, adjoint_in)):
        east_strip = jnp.zeros((HALO_ROWS, LANES), f32)
        west_strip = jnp.zeros((HALO_ROWS, LANES), f32)
        for plane in range(PLANES + 1 - kind):
            if plane < PLANES:
                f, l = plane // LEVB, plane % LEVB
                at = kind * PLANES + plane
                own_w, own_e = source[f, l, :, 0:LANES], source[f, l, :, LANES:]
            else:
                at = 2 * PLANES
                own_w, own_e = mask[:, 0:LANES].astype(f32), mask[:, LANES:].astype(f32)
            edge_w = jnp.concatenate([own_w, from_north[at, :, 0:LANES], from_south[at, :, 0:LANES]], axis=0)
            edge_e = jnp.concatenate([own_e, from_north[at, :, LANES:], from_south[at, :, LANES:]], axis=0)
            east_strip = jnp.where(lane_group == plane, pltpu.roll(edge_e, 8 * plane + 8, 1), east_strip)
            moved = edge_w if plane == 0 else pltpu.roll(edge_w, 8 * plane, 1)
            west_strip = jnp.where(lane_group == plane, moved, west_strip)
        to_east[kind] = east_strip
        to_west[kind] = west_strip


def to_adjoint_rows(x):
    row = iota((8, WIDE), 0)
    return jnp.concatenate([x[0:ROWS], jnp.where(row < 4, x[ROWS : ROWS + 8], x[ROWS + 8 :])], axis=0)


def forward_kernel(
    place,
    diffusivity,
    checkpoint,
    adjoint_in,
    mask,
    from_south,
    from_north,
    from_west,
    from_east,
    wet_out,
    start,
    speed_e,
    speed_n,
    grad_e,
    grad_n,
    early_e,
    early_n,
    base,
    state,
    wet_all,
    spare,
    spare_e,
    spare_n,
):
    @pl.when(place[0] == 3)
    def _():
        t = jnp.tanh(checkpoint[...])
        base[...] = adjoint_in[...] * (1.0 - t * t)

    @pl.when(place[0] != 3)
    def _():
        lane = iota((HALO_ROWS, LANES), 1)

        def widened(own, at, kind, plane):
            full = jnp.concatenate([own, from_north[at], from_south[at]], axis=0)
            low, high = from_east[kind], from_west[kind]
            if plane:
                low = pltpu.roll(low, LANES - 8 * plane, 1)
            high = pltpu.roll(high, (120 - 8 * plane) % LANES, 1)
            edge = jnp.where(lane < 8, low, jnp.where(lane >= 120, high, 0.0))
            return jnp.concatenate([full, edge], axis=1)

        wet = widened(mask[...].astype(f32), 2 * PLANES, 0, PLANES)
        wet_all[...] = wet
        wet_out[...] = to_adjoint_rows(wet)
        for f in range(FLD):
            for l in range(LEVB):
                plane = f * LEVB + l
                state[0, plane] = widened(checkpoint[f, l], plane, 0, plane)
                adj = to_adjoint_rows(widened(adjoint_in[f, l], PLANES + plane, 1, plane))
                if f < NFLUX:
                    start[f, l] = adj
                else:
                    spare[f - NFLUX, l] = adj

        def sweep(step, last):
            now, later = step % 2, (step + 1) % 2
            for l in range(LEVB):
                a = 0.5 * STEP_COEF * (SPEED_BASE + SPEED_GAIN * state[now, l])
                b = (0.5 * STEP_COEF * SPEED_GAIN) * state[now, LEVB + l]
                speed_e[step, l] = to_adjoint_rows(a)
                speed_n[step, l] = to_adjoint_rows(b)
                for f in range(FLD):
                    d = diffusivity[f]
                    q = state[now, f * LEVB + l]
                    q_e, q_w, q_n, q_s = east(q), west(q), north(q), south(q)
                    across, along = q_e - q_w, q_n - q_s
                    half = -0.5 * STEP_COEF * SPEED_GAIN
                    if f < NFLUX:
                        grad_e[step, f, l] = to_adjoint_rows(half * across)
                        grad_n[step, f, l] = to_adjoint_rows(half * along)
                    else:
                        spare_e[step, f - NFLUX, l] = to_adjoint_rows(half * across)
                        spare_n[step, f - NFLUX, l] = to_adjoint_rows(half * along)
                    if not last:
                        moved = (1.0 - 4.0 * d) * q + d * ((q_e + q_w) + (q_n + q_s)) - a * across - b * along
                        state[later, f * LEVB + l] = wet_all[...] * moved

        for step in range(NSTEP):
            sweep(step, step + 1 == NSTEP)

        for step in reversed(range(NSTEP)):
            for l in range(LEVB):
                a, b, w = speed_e[step, l], speed_n[step, l], wet_out[...]
                sum_e, sum_n = 0.0, 0.0
                for f in range(FLD - NFLUX):
                    d = diffusivity[NFLUX + f]
                    mu = w * spare[f, l]
                    sum_e = sum_e + mu * spare_e[step, f, l]
                    sum_n = sum_n + mu * spare_n[step, f, l]
                    spare[f, l] = pulled(mu, a, b, d)
                early_e[step, l] = sum_e
                early_n[step, l] = sum_n
        for f in range(FLD - NFLUX):
            for l in range(LEVB):
                base[NFLUX + f, l] = spare[f, l, 0:ROWS, 0:COLS]


def pulled(mu, a, b, d):
    mixed, carried_e, carried_n = d * mu, a * mu, b * mu
    return (
        (1.0 - 4.0 * d) * mu
        + (east(mixed + carried_e) + west(mixed - carried_e))
        + (north(mixed + carried_n) + south(mixed - carried_n))
    )


def route_kernel(place, table, routing, high, low, spread_own, spread_side, code_t, prof_t, total):
    lat_me, lon_me = place[1], place[2]

    def listed(at):
        return jnp.concatenate(
            [routing[pl.ds(2 * at, TILES, stride=8), :], routing[pl.ds(2 * at + 1, TILES, stride=8), :]], axis=0
        )

    dest, row, profile = listed(0), listed(1), listed(2)
    dest_lat, dest_lon = dest // 16, dest % 16
    row = row + ROWS * (dest_lat - lat_me)
    valid = jnp.logical_and(row >= -4, row < ROWS + 4)
    code = jnp.where(row < 0, row + ADJ_ROWS, row).astype(f32)
    for way in range(3):
        lon_of = (lon_me + (0, 1, 15)[way]) % 16
        here = jnp.logical_and(valid, dest_lon == lon_of)
        code_t[way] = jnp.where(here, code, FAR).T
    for c in range(4):
        weights = jnp.zeros((LANES, LANES), f32)
        for w in range(8):
            weights = jnp.where(profile == w, table[w, c], weights)
        prof_t[c] = weights.T
    rows = iota((ADJ_ROWS, LANES), 0).astype(f32)

    def build(step, carry):
        way, seg = step // 8, step % 8
        sums = [jnp.zeros((ADJ_ROWS, LANES), f32) for _ in range(4)]
        for r in range(16):
            at = seg * 16 + r
            hit = code_t[way, pl.ds(at, 1), :] == rows
            for c in range(4):
                sums[c] = sums[c] + jnp.where(hit, prof_t[c, pl.ds(at, 1), :], 0.0)
        for c in range(4):
            total[seg, way * 4 + c] = sums[c]
        return carry

    lax.fori_loop(0, 24, build, 0)
    for seg in range(8):
        whole = total[seg].reshape(12 * ADJ_ROWS, LANES)
        head, tail = split(whole)
        high[:, seg * LANES : (seg + 1) * LANES] = head
        low[:, seg * LANES : (seg + 1) * LANES] = tail

    src, out = iota((512, 512), 0), iota((512, 512), 1)
    same = (src // 64) % 2 == out // COLS
    spread_own[...] = jnp.where(jnp.logical_and(same, out % COLS == 4 * (src % 64) + src // 128), 1.0, 0.0).astype(bf16)
    src, out = iota((512, 256), 0), iota((512, 256), 1)
    same = (src // 64) % 2 == out // LANES
    first = jnp.logical_and(src % 64 == 0, out % LANES == src // 128)
    final = jnp.logical_and(src % 64 == 63, out % LANES == 124 + src // 128)
    spread_side[...] = jnp.where(jnp.logical_and(same, jnp.logical_or(first, final)), 1.0, 0.0).astype(bf16)


def adjoint_kernel(
    place,
    diffusivity,
    penetration,
    gathered,
    high,
    low,
    spread_own,
    spread_side,
    wet,
    start,
    speed_e,
    speed_n,
    grad_e,
    grad_n,
    early_e,
    early_n,
    base,
    out,
    g_high,
    g_low,
    lam,
    done,
    sem,
):
    del base

    @pl.when(place[0] != 3)
    def _():
        for seg in range(8):
            for h in range(2):
                s = h * 8 + seg
                at = (s % 4) * 4 + s // 4
                for half in range(2):
                    part = gathered[pl.ds(half * 16 + at, TILES, stride=32), :]
                    head, tail = split(part)
                    rows = slice(seg * LANES + h * 64, seg * LANES + h * 64 + 64)
                    g_high[rows, half * LANES : (half + 1) * LANES] = head
                    g_low[rows, half * LANES : (half + 1) * LANES] = tail
        coarse = dot(high[...], g_high[...]) + dot(high[...], g_low[...]) + dot(low[...], g_high[...])
        own_parts, side_parts = [], []
        lane = iota((ADJ_ROWS, LANES), 1) % 64
        for half in range(2):
            cols = slice(half * LANES, (half + 1) * LANES)

            def piece(way, c):
                at = (way * 4 + c) * ADJ_ROWS
                return coarse[at : at + ADJ_ROWS, cols]

            own = jnp.concatenate([piece(0, c) for c in range(4)], axis=1)
            side = jnp.concatenate(
                [jnp.where(lane == 0, piece(1, c), jnp.where(lane == 63, piece(2, c), 0.0)) for c in range(4)], axis=1
            )
            for parts, value in ((own_parts, own), (side_parts, side)):
                head = value.astype(bf16).astype(f32)
                parts += [head, value - head]
        own = dot(jnp.concatenate(own_parts, axis=0).astype(bf16), spread_own[...])
        side = dot(jnp.concatenate(side_parts, axis=0).astype(bf16), spread_side[...])
        w = wet[...]
        band = jnp.minimum(place[0], 2)
        for k in range(NFLUX):
            at, sub = (k // 2) * 2 * ADJ_ROWS, k % 2
            own_k = own[:, sub * COLS : (sub + 1) * COLS]
            side_k = side[:, sub * LANES : (sub + 1) * LANES]
            whole = jnp.concatenate(
                [x[at : at + ADJ_ROWS] + x[at + ADJ_ROWS : at + 2 * ADJ_ROWS] for x in (own_k, side_k)], axis=1
            )
            forcing = w * whole
            for l in range(LEVB):
                lam[k, l] = start[k, l] + penetration[band * LEVB + l] * forcing

        def back(i, carry):
            step = NSTEP - 1 - i
            for l in range(LEVB):
                a, b, w = speed_e[step, l], speed_n[step, l], wet[...]
                sum_e, sum_n = early_e[step, l], early_n[step, l]
                for f in (2, 3, 1, 0):
                    mu = w * lam[f, l]
                    sum_e = sum_e + mu * grad_e[step, f, l]
                    sum_n = sum_n + mu * grad_n[step, f, l]
                    lam[f, l] = pulled(mu, a, b, diffusivity[f])
                lam[0, l] = lam[0, l] + sum_e
                lam[1, l] = lam[1, l] + sum_n
            return carry

        lax.fori_loop(0, NSTEP, back, 0)
        for k in range(NFLUX):
            for l in range(LEVB):
                done[k, l] = lam[k, l, 0:ROWS, 0:COLS]
        copy = pltpu.make_async_copy(done, out.at[0:NFLUX], sem)
        copy.start()
        copy.wait()


def shards(
    checkpoint,
    adjoint_in,
    land_mask,
    diffusivity,
    penetration,
    column_weight,
    routes,
    dest_row,
    weight_id,
    regrid_table,
):
    comp, lat, lon = lax.axis_index("comp"), lax.axis_index("lat"), lax.axis_index("lon")
    place = jnp.stack([comp, lat, lon]).astype(jnp.int32)
    state, adj = checkpoint[0], adjoint_in[0]
    spread_weight = jnp.repeat(column_weight, 4, axis=1)
    own_row = iota((1, 4, PLANES * ROWS), 2) % 4 == iota((1, 4, PLANES * ROWS), 1)
    weight = jnp.where(own_row, spread_weight[:, None, :], 0.0).reshape(16, PLANES * ROWS)

    routing = jnp.concatenate(
        [routes.reshape(2, LANES), dest_row.reshape(2, LANES), weight_id.reshape(2, LANES), jnp.zeros((2, LANES), jnp.int32)]
    )
    edge = jax.ShapeDtypeStruct((2 * PLANES + 1, 8, COLS), f32)
    flux, to_north, to_south = pl.pallas_call(
        flux_kernel,
        out_shape=(jax.ShapeDtypeStruct((32, LANES), f32), edge, edge),
        in_specs=[smem()] + [vmem()] * 4,
        out_specs=(vmem(),) * 3,
        compiler_params=pltpu.CompilerParams(vmem_limit_bytes=12 << 20),
        name="flux",
    )(place, state, adj, land_mask, weight)
    sent = [lax.ppermute(flux, "comp", [(3, band)]) for band in range(3)]
    from_south = lax.ppermute(to_north, "lat", [(i, i + 1) for i in range(3)])
    from_north = lax.ppermute(to_south, "lat", [(i + 1, i) for i in range(3)])
    routing_all = lax.all_to_all(
        jnp.broadcast_to(routing[None], (TILES, 8, LANES)), ("lat", "lon"), split_axis=0, concat_axis=0, tiled=True
    ).reshape(TILES * 8, LANES)

    strip = jax.ShapeDtypeStruct((2, HALO_ROWS, LANES), f32)
    to_east, to_west = pl.pallas_call(
        strip_kernel,
        out_shape=(strip, strip),
        in_specs=[vmem()] * 5,
        out_specs=(vmem(),) * 2,
        compiler_params=pltpu.CompilerParams(vmem_limit_bytes=12 << 20),
        name="strips",
    )(state, adj, land_mask, from_south, from_north)
    from_west = lax.ppermute(to_east, "lon", [(i, (i + 1) % 16) for i in range(16)])
    from_east = lax.ppermute(to_west, "lon", [((i + 1) % 16, i) for i in range(16)])

    here = jnp.where(comp == 3, flux, sent[0] + sent[1] + sent[2])
    flux_all = lax.all_to_all(
        jnp.broadcast_to(here[None], (TILES, 32, LANES)), ("lat", "lon"), split_axis=0, concat_axis=0, tiled=True
    ).reshape(TILES * 32, LANES)

    high, low, spread_own, spread_side = pl.pallas_call(
        route_kernel,
        out_shape=(
            in_vmem((12 * ADJ_ROWS, 1024), bf16),
            in_vmem((12 * ADJ_ROWS, 1024), bf16),
            in_vmem((512, 512), bf16),
            in_vmem((512, 256), bf16),
        ),
        in_specs=[smem(), smem(), vmem()],
        out_specs=(vmem(),) * 4,
        scratch_shapes=[
            VM((3, LANES, LANES), f32),
            VM((4, LANES, LANES), f32),
            VM((8, 12, ADJ_ROWS, LANES), f32),
        ],
        compiler_params=pltpu.CompilerParams(vmem_limit_bytes=16 << 20),
        name="routing",
    )(place, regrid_table, routing_all)

    wide = (ADJ_ROWS, WIDE)
    prepared = pl.pallas_call(
        forward_kernel,
        out_shape=(
            in_vmem(wide),
            in_vmem((NFLUX, LEVB) + wide),
            in_vmem((NSTEP, LEVB) + wide),
            in_vmem((NSTEP, LEVB) + wide),
            in_vmem((NSTEP, NFLUX, LEVB) + wide),
            in_vmem((NSTEP, NFLUX, LEVB) + wide),
            in_vmem((NSTEP, LEVB) + wide),
            in_vmem((NSTEP, LEVB) + wide),
            jax.ShapeDtypeStruct((FLD, LEVB, ROWS, COLS), f32),
        ),
        in_specs=[smem(), smem()] + [vmem()] * 7,
        out_specs=(vmem(),) * 9,
        scratch_shapes=[
            VM((2, PLANES, HALO_ROWS, WIDE), f32),
            VM((HALO_ROWS, WIDE), f32),
            VM((FLD - NFLUX, LEVB) + wide, f32),
            VM((NSTEP, FLD - NFLUX, LEVB) + wide, f32),
            VM((NSTEP, FLD - NFLUX, LEVB) + wide, f32),
        ],
        compiler_params=pltpu.CompilerParams(vmem_limit_bytes=32 << 20),
        name="forward",
    )(place, diffusivity, state, adj, land_mask, from_south, from_north, from_west, from_east)
    base = prepared[8]

    result = pl.pallas_call(
        adjoint_kernel,
        out_shape=jax.ShapeDtypeStruct((FLD, LEVB, ROWS, COLS), f32),
        in_specs=[smem()] * 3 + [vmem()] * 13 + [pl.BlockSpec(memory_space=pl.ANY)],
        out_specs=pl.BlockSpec(memory_space=pl.ANY),
        scratch_shapes=[
            VM((1024, COLS), bf16),
            VM((1024, COLS), bf16),
            VM((NFLUX, LEVB) + wide, f32),
            VM((NFLUX, LEVB, ROWS, COLS), f32),
            pltpu.SemaphoreType.DMA,
        ],
        input_output_aliases={16: 0},
        compiler_params=pltpu.CompilerParams(vmem_limit_bytes=32 << 20),
        name="adjoint",
    )(place, diffusivity, penetration, flux_all, high, low, spread_own, spread_side, *prepared[:8], base)
    return result[None]


def solution(mesh):
    in_specs = (
        P("comp", None, None, "lat", "lon"),
        P("comp", None, None, "lat", "lon"),
        P("lat", "lon"),
        P(),
        P(),
        P(),
        P(("lat", "lon"), None),
        P(("lat", "lon")),
        P(("lat", "lon")),
        P(),
    )
    out_specs = P("comp", None, None, "lat", "lon")
    return jax.shard_map(shards, mesh=mesh, in_specs=in_specs, out_specs=out_specs, check_vma=False)
```

```python
import jax
import jax.numpy as jnp
import ml_dtypes
import numpy as np
from jax import lax
from jax.experimental import pallas as pl
from jax.experimental.pallas import tpu as pltpu
from jax.sharding import PartitionSpec as P

NSTEP = 4
STEP_COEF = 0.2
SPEED_BASE = 0.5
SPEED_GAIN = 0.5

FLD = 6
NFLUX = 4
LEVB = 2
ROWS = 64
COLS = 256
PLANES = FLD * LEVB
HALO_ROWS = 80
ADJ_ROWS = 72
WIDE = 384
LANES = 128
TILES = 64
SEGS = 16
FAR = -1.0

f32 = jnp.float32
bf16 = jnp.bfloat16
VM = pltpu.VMEM
SM = pltpu.SMEM


def vmem():
    return pl.BlockSpec(memory_space=VM)


def smem():
    return pl.BlockSpec(memory_space=SM)


def in_hbm():
    return pl.BlockSpec(memory_space=pltpu.HBM)


def hbm(x):
    return pltpu.with_memory_space_constraint(jnp.asarray(x), pltpu.HBM)


def shape_of(shape, dtype=f32):
    return jax.ShapeDtypeStruct(shape, dtype)


def east(x):
    return pltpu.roll(x, WIDE - 1, 1)


def west(x):
    return pltpu.roll(x, 1, 1)


def north(x):
    return pltpu.roll(x, x.shape[0] - 1, 0)


def south(x):
    return pltpu.roll(x, 1, 0)


def iota(shape, dim):
    return lax.broadcasted_iota(jnp.int32, shape, dim)


def split(x):
    high = x.astype(bf16)
    return high, (x - high.astype(f32)).astype(bf16)


def dot(x, y):
    return jnp.dot(x, y, preferred_element_type=f32)


def flux_kernel(
    checkpoint, adjoint_in, mask, weight, flux, to_north, to_south, held, held_adj, held_mask, held_weight, sems
):
    copies = [
        pltpu.make_async_copy(source, target, sems.at[at])
        for at, (source, target) in enumerate(
            ((checkpoint, held), (adjoint_in, held_adj), (mask, held_mask), (weight, held_weight))
        )
    ]
    for copy in copies:
        copy.start()
    copies[3].wait()
    atmosphere = lax.axis_index("comp") == 3

    @pl.when(atmosphere)
    def _():
        w = held_weight[...]
        head = w.astype(bf16).astype(f32)
        rest = w - head
        middle = rest.astype(bf16).astype(f32)
        parts = jnp.concatenate([head, middle, rest - middle, jnp.zeros_like(w)], axis=0).astype(bf16)
        level, row = iota((FLD * 32, PLANES * ROWS), 0), iota((FLD * 32, PLANES * ROWS), 1)
        repeated = dot(parts, jnp.where(row // 4 == level, 1.0, 0.0).astype(bf16))
        repeated = repeated[0:4] + repeated[4:8] + repeated[8:12]
        own = iota((4, PLANES * ROWS), 1) % 4 == iota((4, PLANES * ROWS), 0)
        spread = jnp.concatenate([jnp.where(own, repeated[k : k + 1], 0.0) for k in range(NFLUX)], axis=0)
        for copy in copies[:3]:
            copy.wait()
        t = jnp.tanh(held[...])
        sens = (held_adj[...] * (1.0 - t * t)).reshape(PLANES * ROWS, COLS)
        by_kind = jnp.dot(spread, sens, precision=lax.Precision.HIGHEST, preferred_element_type=f32)
        rows = []
        for q in range(4):
            rows.append(
                jnp.concatenate(
                    [by_kind[k * 4 : k * 4 + 4, q * 64 : q * 64 + 64] for k in range(NFLUX)], axis=1
                )
            )
        by_seg = jnp.concatenate(rows, axis=0)
        flux[0:16, :] = by_seg[:, 0:LANES]
        flux[16:32, :] = by_seg[:, LANES:]

    @pl.when(jnp.logical_not(atmosphere))
    def _():
        flux[...] = jnp.zeros((32, LANES), f32)
        for copy in copies[:3]:
            copy.wait()
        for plane in range(PLANES):
            f, l = plane // LEVB, plane % LEVB
            to_north[plane] = held[f, l, ROWS - 8 : ROWS, :]
            to_south[plane] = held[f, l, 0:8, :]
            to_north[PLANES + plane] = held_adj[f, l, ROWS - 8 : ROWS, :]
            to_south[PLANES + plane] = held_adj[f, l, 0:8, :]
        to_north[2 * PLANES] = held_mask[ROWS - 8 : ROWS, :].astype(f32)
        to_south[2 * PLANES] = held_mask[0:8, :].astype(f32)


def payload_kernel(flux, first, second, third, routes, dest_row, weight_id, from_south, from_north, payload):
    del from_south, from_north
    whole = flux[...] + (first[...] + second[...] + third[...])
    listing = [x[...].astype(f32) for x in (routes, dest_row, weight_id)]
    listing = jnp.concatenate(listing + [jnp.zeros((2, LANES), f32)], axis=0)

    def copy_out(tile, carry):
        payload[tile, 0:32, :] = whole
        payload[tile, 32:40, :] = listing
        return carry

    lax.fori_loop(0, TILES, copy_out, 0)


def strip_kernel(checkpoint, adjoint_in, mask, from_south, from_north, to_east, to_west):
    lane_group = iota((HALO_ROWS, LANES), 1) // 8
    for kind, source in enumerate((checkpoint, adjoint_in)):
        east_strip = jnp.zeros((HALO_ROWS, LANES), f32)
        west_strip = jnp.zeros((HALO_ROWS, LANES), f32)
        for plane in range(PLANES + 1 - kind):
            if plane < PLANES:
                f, l = plane // LEVB, plane % LEVB
                at = kind * PLANES + plane
                own_w, own_e = source[f, l, :, 0:LANES], source[f, l, :, LANES:]
            else:
                at = 2 * PLANES
                own_w, own_e = mask[:, 0:LANES].astype(f32), mask[:, LANES:].astype(f32)
            edge_w = jnp.concatenate([own_w, from_north[at, :, 0:LANES], from_south[at, :, 0:LANES]], axis=0)
            edge_e = jnp.concatenate([own_e, from_north[at, :, LANES:], from_south[at, :, LANES:]], axis=0)
            east_strip = jnp.where(lane_group == plane, pltpu.roll(edge_e, 8 * plane + 8, 1), east_strip)
            moved = edge_w if plane == 0 else pltpu.roll(edge_w, 8 * plane, 1)
            west_strip = jnp.where(lane_group == plane, moved, west_strip)
        to_east[kind] = east_strip
        to_west[kind] = west_strip


def to_adjoint_rows(x):
    row = iota((8, WIDE), 0)
    return jnp.concatenate([x[0:ROWS], jnp.where(row < 4, x[ROWS : ROWS + 8], x[ROWS + 8 :])], axis=0)


def pulled(mu, a, b, d):
    mixed, carried_e, carried_n = d * mu, a * mu, b * mu
    return (
        (1.0 - 4.0 * d) * mu
        + (east(mixed + carried_e) + west(mixed - carried_e))
        + (north(mixed + carried_n) + south(mixed - carried_n))
    )


def route_matrix(gathered, table, high, low, code_t, prof_t, total):
    lat_me, lon_me = lax.axis_index("lat"), lax.axis_index("lon")

    def listed(at):
        parts = [gathered[pl.ds(32 + 2 * at + half, TILES, stride=40), :] for half in range(2)]
        return jnp.concatenate(parts, axis=0).astype(jnp.int32)

    dest, row, profile = listed(0), listed(1), listed(2)
    dest_lat, dest_lon = dest // 16, dest % 16
    row = row + ROWS * (dest_lat - lat_me)
    valid = jnp.logical_and(row >= -4, row < ROWS + 4)
    code = jnp.where(row < 0, row + ADJ_ROWS, row).astype(f32)
    for way in range(3):
        lon_of = (lon_me + (0, 1, 15)[way]) % 16
        here = jnp.logical_and(valid, dest_lon == lon_of)
        code_t[way] = jnp.where(here, code, FAR).T
    for c in range(4):
        weights = jnp.zeros((LANES, LANES), f32)
        for w in range(8):
            weights = jnp.where(profile == w, table[c, w], weights)
        prof_t[c] = weights.T
    rows = iota((ADJ_ROWS, LANES), 0).astype(f32)

    def build(step, carry):
        way, seg = step // 8, step % 8
        sums = [jnp.zeros((ADJ_ROWS, LANES), f32) for _ in range(4)]
        for r in range(16):
            at = seg * 16 + r
            hit = code_t[way, pl.ds(at, 1), :] == rows
            for c in range(4):
                sums[c] = sums[c] + jnp.where(hit, prof_t[c, pl.ds(at, 1), :], 0.0)
        for c in range(4):
            total[seg, way * 4 + c] = sums[c]
        return carry

    lax.fori_loop(0, 24, build, 0)
    for seg in range(8):
        whole = total[seg].reshape(12 * ADJ_ROWS, LANES)
        head, tail = split(whole)
        high[:, seg * LANES : (seg + 1) * LANES] = head
        low[:, seg * LANES : (seg + 1) * LANES] = tail


def spread_tables():
    src, out = np.arange(512)[:, None], np.arange(512)[None, :]
    own = ((src // 64) % 2 == out // COLS) & (out % COLS == 4 * (src % 64) + src // 128)
    out = np.arange(256)[None, :]
    first = (src % 64 == 0) & (out % LANES == src // 128)
    final = (src % 64 == 63) & (out % LANES == 124 + src // 128)
    side = ((src // 64) % 2 == out // LANES) & (first | final)
    return own.astype(ml_dtypes.bfloat16), side.astype(ml_dtypes.bfloat16)


def assemble_forcing(gathered, high, low, g_high, g_low, spread_own, spread_side):
    for seg in range(8):
        for h in range(2):
            s = h * 8 + seg
            at = (s % 4) * 4 + s // 4
            for half in range(2):
                part = gathered[pl.ds(half * 16 + at, TILES, stride=40), :]
                head, tail = split(part)
                rows = slice(seg * LANES + h * 64, seg * LANES + h * 64 + 64)
                g_high[rows, half * LANES : (half + 1) * LANES] = head
                g_low[rows, half * LANES : (half + 1) * LANES] = tail
    coarse = dot(high[...], g_high[...]) + dot(high[...], g_low[...]) + dot(low[...], g_high[...])
    own_parts, side_parts = [], []
    lane = iota((ADJ_ROWS, LANES), 1) % 64
    for half in range(2):
        cols = slice(half * LANES, (half + 1) * LANES)

        def piece(way, c):
            at = (way * 4 + c) * ADJ_ROWS
            return coarse[at : at + ADJ_ROWS, cols]

        own = jnp.concatenate([piece(0, c) for c in range(4)], axis=1)
        side = jnp.concatenate(
            [jnp.where(lane == 0, piece(1, c), jnp.where(lane == 63, piece(2, c), 0.0)) for c in range(4)], axis=1
        )
        for parts, value in ((own_parts, own), (side_parts, side)):
            head = value.astype(bf16).astype(f32)
            parts += [head, value - head]
    own = dot(jnp.concatenate(own_parts, axis=0).astype(bf16), spread_own[...])
    side = dot(jnp.concatenate(side_parts, axis=0).astype(bf16), spread_side[...])
    return own, side


def forward_steps(state, wet_all, diffusivity, speed_e, speed_n, grad_e, grad_n):
    for step in range(NSTEP):
        now, later = step % 2, (step + 1) % 2
        for l in range(LEVB):
            a = 0.5 * STEP_COEF * (SPEED_BASE + SPEED_GAIN * state[now, l])
            b = (0.5 * STEP_COEF * SPEED_GAIN) * state[now, LEVB + l]
            speed_e[step, l] = to_adjoint_rows(a)
            speed_n[step, l] = to_adjoint_rows(b)
            for f in range(FLD):
                d = diffusivity[f]
                q = state[now, f * LEVB + l]
                q_e, q_w, q_n, q_s = east(q), west(q), north(q), south(q)
                across, along = q_e - q_w, q_n - q_s
                half = -0.5 * STEP_COEF * SPEED_GAIN
                grad_e[step, f, l] = to_adjoint_rows(half * across)
                grad_n[step, f, l] = to_adjoint_rows(half * along)
                if step + 1 < NSTEP:
                    moved = (1.0 - 4.0 * d) * q + d * ((q_e + q_w) + (q_n + q_s)) - a * across - b * along
                    state[later, f * LEVB + l] = wet_all[...] * moved


def ocean_kernel(
    diffusivity_at,
    penetration_at,
    table_at,
    spread_own_at,
    spread_side_at,
    checkpoint,
    adjoint_in,
    mask,
    from_south,
    from_north,
    from_west,
    from_east,
    gathered,
    out,
    diffusivity,
    penetration,
    table,
    spread_own,
    spread_side,
    mask_own,
    state,
    lam,
    wet_all,
    wet,
    speed_e,
    speed_n,
    grad_e,
    grad_n,
    high,
    low,
    code_t,
    prof_t,
    total,
    g_high,
    g_low,
    done,
    sems,
):
    section = lax.axis_index("comp")
    pairs = [
        (diffusivity_at, diffusivity),
        (penetration_at, penetration),
        (table_at, table),
        (spread_own_at, spread_own),
        (spread_side_at, spread_side),
        (mask, mask_own),
    ]
    for plane in range(PLANES):
        f, l = plane // LEVB, plane % LEVB
        pairs.append((checkpoint.at[f, l], state.at[0, plane, 0:ROWS, 0:COLS]))
        pairs.append((adjoint_in.at[f, l], lam.at[f, l, 0:ROWS, 0:COLS]))
    copies = [pltpu.make_async_copy(source, target, sems.at[at]) for at, (source, target) in enumerate(pairs)]
    for copy in copies:
        copy.start()

    @pl.when(section == 3)
    def _():
        for copy in copies:
            copy.wait()
        for plane in range(PLANES):
            f, l = plane // LEVB, plane % LEVB
            t = jnp.tanh(state[0, plane, 0:ROWS, 0:COLS])
            done[f, l] = lam[f, l, 0:ROWS, 0:COLS] * (1.0 - t * t)

    @pl.when(section != 3)
    def _():
        for copy in copies[:3]:
            copy.wait()
        route_matrix(gathered, table, high, low, code_t, prof_t, total)
        for copy in copies[3:]:
            copy.wait()
        own, side = assemble_forcing(gathered, high, low, g_high, g_low, spread_own, spread_side)

        lane = iota((HALO_ROWS, LANES), 1)

        def edge(kind, plane):
            west_side, east_side = from_west[kind], from_east[kind]
            if plane:
                east_side = pltpu.roll(east_side, LANES - 8 * plane, 1)
            west_side = pltpu.roll(west_side, (120 - 8 * plane) % LANES, 1)
            return jnp.where(lane < 8, east_side, jnp.where(lane >= 120, west_side, 0.0))

        def rows_between(at):
            row = iota((8, COLS), 0)
            return jnp.where(row < 4, from_north[at], from_south[at])

        at = 2 * PLANES
        wet_all[0:ROWS, 0:COLS] = mask_own[...].astype(f32)
        wet_all[ROWS : ROWS + 8, 0:COLS] = from_north[at]
        wet_all[ROWS + 8 :, 0:COLS] = from_south[at]
        wet_all[:, COLS:] = edge(0, PLANES)
        wet[...] = to_adjoint_rows(wet_all[...])
        row8 = iota((8, LANES), 0)
        for f in range(FLD):
            for l in range(LEVB):
                plane = f * LEVB + l
                state[0, plane, ROWS : ROWS + 8, 0:COLS] = from_north[plane]
                state[0, plane, ROWS + 8 :, 0:COLS] = from_south[plane]
                state[0, plane, :, COLS:] = edge(0, plane)
                lam[f, l, ROWS:, 0:COLS] = rows_between(PLANES + plane)
                side_col = edge(1, plane)
                lam[f, l, 0:ROWS, COLS:] = side_col[0:ROWS]
                lam[f, l, ROWS:, COLS:] = jnp.where(row8 < 4, side_col[ROWS : ROWS + 8], side_col[ROWS + 8 :])
        w = wet[...]
        band = jnp.minimum(section, 2)
        for k in range(NFLUX):
            at, sub = (k // 2) * 2 * ADJ_ROWS, k % 2
            own_k = own[:, sub * COLS : (sub + 1) * COLS]
            side_k = side[:, sub * LANES : (sub + 1) * LANES]
            whole = jnp.concatenate(
                [x[at : at + ADJ_ROWS] + x[at + ADJ_ROWS : at + 2 * ADJ_ROWS] for x in (own_k, side_k)], axis=1
            )
            forcing = w * whole
            for l in range(LEVB):
                lam[k, l] = lam[k, l] + penetration[band * LEVB + l] * forcing

        forward_steps(state, wet_all, diffusivity, speed_e, speed_n, grad_e, grad_n)

        def back(i, carry):
            step = NSTEP - 1 - i
            for l in range(LEVB):
                a, b, w = speed_e[step, l], speed_n[step, l], wet[...]
                sum_e, sum_n = 0.0, 0.0
                for f in (2, 3, 4, 5, 1, 0):
                    mu = w * lam[f, l]
                    sum_e = sum_e + mu * grad_e[step, f, l]
                    sum_n = sum_n + mu * grad_n[step, f, l]
                    lam[f, l] = pulled(mu, a, b, diffusivity[f])
                lam[0, l] = lam[0, l] + sum_e
                lam[1, l] = lam[1, l] + sum_n
            return carry

        lax.fori_loop(0, NSTEP, back, 0)
        for f in range(FLD):
            for l in range(LEVB):
                done[f, l] = lam[f, l, 0:ROWS, 0:COLS]

    copy = pltpu.make_async_copy(done, out, sems.at[0])
    copy.start()
    copy.wait()


def shards(
    checkpoint,
    adjoint_in,
    land_mask,
    diffusivity,
    penetration,
    column_weight,
    routes,
    dest_row,
    weight_id,
    regrid_table,
):
    state, adj = checkpoint[0], adjoint_in[0]
    edge = pltpu.HBM((2 * PLANES + 1, 8, COLS), f32)
    flux, to_north, to_south = pl.pallas_call(
        flux_kernel,
        out_shape=(shape_of((32, LANES)), edge, edge),
        in_specs=[in_hbm()] * 4,
        out_specs=(vmem(),) * 3,
        scratch_shapes=[
            VM((FLD, LEVB, ROWS, COLS), f32),
            VM((FLD, LEVB, ROWS, COLS), f32),
            VM((ROWS, COLS), jnp.int32),
            VM((NFLUX, FLD * 32), f32),
            pltpu.SemaphoreType.DMA((4,)),
        ],
        compiler_params=pltpu.CompilerParams(vmem_limit_bytes=12 << 20),
        name="flux",
    )(*[hbm(x) for x in (state, adj, land_mask, column_weight)])
    sent = [lax.ppermute(flux, "comp", [(3, band)]) for band in range(3)]
    from_south = lax.ppermute(to_north, "lat", [(i, i + 1) for i in range(3)])
    from_north = lax.ppermute(to_south, "lat", [(i + 1, i) for i in range(3)])

    strip = shape_of((2, HALO_ROWS, LANES))
    to_east, to_west = pl.pallas_call(
        strip_kernel,
        out_shape=(strip, strip),
        in_specs=[vmem()] * 5,
        out_specs=(vmem(),) * 2,
        compiler_params=pltpu.CompilerParams(vmem_limit_bytes=12 << 20),
        name="strips",
    )(state, adj, land_mask, from_south, from_north)
    from_west = lax.ppermute(to_east, "lon", [(i, (i + 1) % 16) for i in range(16)])
    from_east = lax.ppermute(to_west, "lon", [((i + 1) % 16, i) for i in range(16)])

    pairs = (2, LANES)
    payload = pl.pallas_call(
        payload_kernel,
        out_shape=pltpu.HBM((TILES, 40, LANES), f32),
        in_specs=[vmem()] * 7 + [pl.BlockSpec(memory_space=pl.ANY)] * 2,
        out_specs=vmem(),
        compiler_params=pltpu.CompilerParams(vmem_limit_bytes=4 << 20),
        name="payload",
    )(flux, *sent, routes.reshape(pairs), dest_row.reshape(pairs), weight_id.reshape(pairs), from_south, from_north)
    gathered = lax.all_to_all(payload, ("lat", "lon"), split_axis=0, concat_axis=0, tiled=True)
    gathered = gathered.reshape(TILES * 40, LANES)

    wide = (ADJ_ROWS, WIDE)
    matrix = (12 * ADJ_ROWS, 1024)
    result = pl.pallas_call(
        ocean_kernel,
        out_shape=shape_of((FLD, LEVB, ROWS, COLS)),
        in_specs=[in_hbm()] * 8 + [vmem()] * 5,
        out_specs=pl.BlockSpec(memory_space=pl.ANY),
        scratch_shapes=[
            SM((FLD,), f32),
            SM((FLD,), f32),
            SM((4, 8), f32),
            VM((512, 512), bf16),
            VM((512, 256), bf16),
            VM((ROWS, COLS), jnp.int32),
            VM((2, PLANES, HALO_ROWS, WIDE), f32),
            VM((FLD, LEVB) + wide, f32),
            VM((HALO_ROWS, WIDE), f32),
            VM(wide, f32),
            VM((NSTEP, LEVB) + wide, f32),
            VM((NSTEP, LEVB) + wide, f32),
            VM((NSTEP, FLD, LEVB) + wide, f32),
            VM((NSTEP, FLD, LEVB) + wide, f32),
            VM(matrix, bf16),
            VM(matrix, bf16),
            VM((3, LANES, LANES), f32),
            VM((4, LANES, LANES), f32),
            VM((8, 12, ADJ_ROWS, LANES), f32),
            VM((1024, COLS), bf16),
            VM((1024, COLS), bf16),
            VM((FLD, LEVB, ROWS, COLS), f32),
            pltpu.SemaphoreType.DMA((6 + 2 * PLANES,)),
        ],
        compiler_params=pltpu.CompilerParams(vmem_limit_bytes=48 << 20),
        name="ocean",
    )(
        *[hbm(x) for x in (diffusivity, penetration, regrid_table.T, *spread_tables(), state, adj, land_mask)],
        from_south,
        from_north,
        from_west,
        from_east,
        gathered,
    )
    return result[None]


def solution(mesh):
    in_specs = (
        P("comp", None, None, "lat", "lon"),
        P("comp", None, None, "lat", "lon"),
        P("lat", "lon"),
        P(),
        P(),
        P(),
        P(("lat", "lon"), None),
        P(("lat", "lon")),
        P(("lat", "lon")),
        P(),
    )
    out_specs = P("comp", None, None, "lat", "lon")
    return jax.shard_map(shards, mesh=mesh, in_specs=in_specs, out_specs=out_specs, check_vma=False)
```

```python
import jax
import jax.numpy as jnp
import ml_dtypes
import numpy as np
from jax import lax
from jax.experimental import pallas as pl
from jax.experimental.pallas import tpu as pltpu
from jax.sharding import PartitionSpec as P

NSTEP = 4
STEP_COEF = 0.2
SPEED_BASE = 0.5
SPEED_GAIN = 0.5

FLD = 6
NFLUX = 4
LEVB = 2
ROWS = 64
COLS = 256
PLANES = FLD * LEVB
HALO_ROWS = 80
ADJ_ROWS = 72
WIDE = 384
LANES = 128
TILES = 64
SEGS = 16
FAR = -1.0

f32 = jnp.float32
bf16 = jnp.bfloat16
VM = pltpu.VMEM
SM = pltpu.SMEM


def vmem():
    return pl.BlockSpec(memory_space=VM)


def smem():
    return pl.BlockSpec(memory_space=SM)


def in_hbm():
    return pl.BlockSpec(memory_space=pltpu.HBM)


def hbm(x):
    return pltpu.with_memory_space_constraint(jnp.asarray(x), pltpu.HBM)


def shape_of(shape, dtype=f32):
    return jax.ShapeDtypeStruct(shape, dtype)


def east(x):
    return pltpu.roll(x, WIDE - 1, 1)


def west(x):
    return pltpu.roll(x, 1, 1)


def north(x):
    return pltpu.roll(x, x.shape[0] - 1, 0)


def south(x):
    return pltpu.roll(x, 1, 0)


def iota(shape, dim):
    return lax.broadcasted_iota(jnp.int32, shape, dim)


def split(x):
    high = x.astype(bf16)
    return high, (x - high.astype(f32)).astype(bf16)


def dot(x, y):
    return jnp.dot(x, y, preferred_element_type=f32)


def exact_parts(x):
    head = x.astype(bf16).astype(f32)
    rest = x - head
    middle = rest.astype(bf16).astype(f32)
    return [head, middle, rest - middle]


def packed_strips(planes_west, planes_east):
    lane_group = iota(planes_west[0].shape, 1) // 8
    east_strip = jnp.zeros(planes_west[0].shape, f32)
    west_strip = east_strip
    for plane, (edge_w, edge_e) in enumerate(zip(planes_west, planes_east)):
        east_strip = jnp.where(lane_group == plane, pltpu.roll(edge_e, 8 * plane + 8, 1), east_strip)
        moved = pltpu.roll(edge_w, 8 * plane, 1) if plane else edge_w
        west_strip = jnp.where(lane_group == plane, moved, west_strip)
    return east_strip, west_strip


def flux_kernel(
    checkpoint,
    adjoint_in,
    mask,
    weight,
    flux,
    to_north,
    to_south,
    own_east,
    own_west,
    held,
    held_adj,
    held_mask,
    held_weight,
    sems,
):
    pairs = ((checkpoint, held), (adjoint_in, held_adj), (mask, held_mask), (weight, held_weight))
    copies = [pltpu.make_async_copy(source, target, sems.at[at]) for at, (source, target) in enumerate(pairs)]
    for copy in copies:
        copy.start()

    @pl.when(lax.axis_index("comp") != 3)
    def _():
        flux[...] = jnp.zeros((40, LANES), f32)
        for copy in copies:
            copy.wait()
        top, low = slice(ROWS - 8, ROWS), slice(0, 8)
        row = iota((8, COLS), 0)
        for f in range(FLD):
            for l in range(LEVB):
                to_north[f * LEVB + l] = held[f, l, top, :]
                to_south[f * LEVB + l] = held[f, l, low, :]
            upper = pltpu.roll(held_adj[f, 1, top, :], 4, 0)
            to_north[PLANES + f] = jnp.where(row < 4, upper, held_adj[f, 0, top, :])
            lower = pltpu.roll(held_adj[f, 1, low, :], 4, 0)
            to_south[PLANES + f] = jnp.where(row < 4, held_adj[f, 0, low, :], lower)
        to_north[PLANES + FLD] = held_mask[top, :].astype(f32)
        to_south[PLANES + FLD] = held_mask[low, :].astype(f32)
        for kind, source in enumerate((held, held_adj)):
            planes = [source[plane // LEVB, plane % LEVB] for plane in range(PLANES)]
            if kind == 0:
                planes.append(held_mask[...].astype(f32))
            own_east[kind], own_west[kind] = packed_strips([x[:, 0:LANES] for x in planes], [x[:, LANES:] for x in planes])

    @pl.when(lax.axis_index("comp") == 3)
    def _():
        copies[3].wait()
        w = held_weight[...]
        parts = jnp.concatenate(exact_parts(w) + [jnp.zeros_like(w)], axis=0).astype(bf16)
        level, row = iota((FLD * 32, PLANES * ROWS), 0), iota((FLD * 32, PLANES * ROWS), 1)
        repeated = dot(parts, jnp.where(row // 4 == level, 1.0, 0.0).astype(bf16))
        repeated = repeated[0:4] + repeated[4:8] + repeated[8:12]
        own = iota((4, PLANES * ROWS), 1) % 4 == iota((4, PLANES * ROWS), 0)
        spread = jnp.concatenate([jnp.where(own, repeated[k : k + 1], 0.0) for k in range(NFLUX)], axis=0)
        for copy in copies[:3]:
            copy.wait()
        t = jnp.tanh(held[...])
        sens = (held_adj[...] * (1.0 - t * t)).reshape(PLANES * ROWS, COLS)
        by_kind = jnp.dot(spread, sens, precision=lax.Precision.HIGHEST, preferred_element_type=f32)
        rows = []
        for q in range(4):
            rows.append(
                jnp.concatenate(
                    [by_kind[k * 4 : k * 4 + 4, q * 64 : q * 64 + 64] for k in range(NFLUX)], axis=1
                )
            )
        by_seg = jnp.concatenate(rows, axis=0)
        flux[0:16, :] = by_seg[:, 0:LANES]
        flux[16:32, :] = by_seg[:, LANES:]
        lane = iota((COLS, LANES), 1)
        pick = jnp.where(iota((COLS, LANES), 0) == (lane % 4) * 64 + 63 * (lane // 64), 1.0, 0.0).astype(bf16)
        ends = dot(jnp.concatenate(exact_parts(by_kind), axis=0).astype(bf16), pick)
        ends = ends[0:16] + ends[16:32] + ends[32:48]
        lane = iota((16, LANES), 1)
        mine = iota((16, LANES), 0) == (lane // 16 % 4) * 4 + lane // 4 % 4
        flux[32:33, :] = jnp.sum(jnp.where(mine, ends, 0.0), axis=0, keepdims=True)
        flux[33:40, :] = jnp.zeros((7, LANES), f32)


def adjoint_halo(from_north, from_south, f, l):
    high, low = from_north[PLANES + f], from_south[PLANES + f]
    if l:
        high, low = pltpu.roll(high, 4, 0), pltpu.roll(low, 4, 0)
    return jnp.where(iota((8, COLS), 0) < 4, high, low)


def strip_kernel(own_east, own_west, from_south, from_north, to_east, to_west):
    states = [jnp.concatenate([from_north[p], from_south[p]], axis=0) for p in range(PLANES)]
    states.append(jnp.concatenate([from_north[PLANES + FLD], from_south[PLANES + FLD]], axis=0))
    adjoints = [adjoint_halo(from_north, from_south, p // LEVB, p % LEVB) for p in range(PLANES)]
    for target, own in ((to_east, own_east), (to_west, own_west)):
        target[0:ROWS, :] = own[0]
        target[HALO_ROWS : HALO_ROWS + ROWS, :] = own[1]
    for start, planes in ((ROWS, states), (HALO_ROWS + ROWS, adjoints)):
        rows = slice(start, start + planes[0].shape[0])
        to_east[rows, :], to_west[rows, :] = packed_strips([x[:, 0:LANES] for x in planes], [x[:, LANES:] for x in planes])


def payload_kernel(flux, first, second, third, routes, dest_row, weight_id, south, north, payload, block, lists, sems):
    del south, north
    copies = [
        pltpu.make_async_copy(x, lists.at[pl.ds(2 * at, 2)], sems.at[at])
        for at, x in enumerate((routes, dest_row, weight_id))
    ]
    for copy in copies:
        copy.start()
    block[...] = flux[...] + (first[...] + second[...] + third[...])
    for copy in copies:
        copy.wait()
    block[33:39, :] = lists[0:6, :].astype(f32)
    copies = [pltpu.make_async_copy(block, payload.at[tile], sems.at[tile]) for tile in range(TILES)]
    for copy in copies:
        copy.start()
    for copy in copies:
        copy.wait()


def to_adjoint_rows(x):
    row = iota((8, WIDE), 0)
    return jnp.concatenate([x[0:ROWS], jnp.where(row < 4, x[ROWS : ROWS + 8], x[ROWS + 8 :])], axis=0)


def pulled(mu, a, b, d):
    mixed, carried_e, carried_n = d * mu, a * mu, b * mu
    return (
        (1.0 - 4.0 * d) * mu
        + (east(mixed + carried_e) + west(mixed - carried_e))
        + (north(mixed + carried_n) + south(mixed - carried_n))
    )


def route_matrix(gathered, table, widen, high, low, code_t, prof_t, total, products, side_code):
    lat_me, lon_me = lax.axis_index("lat"), lax.axis_index("lon")

    def listed(at):
        parts = [gathered[pl.ds(33 + 2 * at + half, TILES, stride=40), :] for half in range(2)]
        return jnp.concatenate(parts, axis=1).astype(jnp.int32)

    def stacked(x):
        return jnp.concatenate([x[:, 0:LANES], x[:, LANES:]], axis=0)

    dest, row, profile = listed(0), listed(1), listed(2)
    dest_lat, dest_lon = jnp.right_shift(dest, 4), jnp.bitwise_and(dest, 15)
    row = row + ROWS * (dest_lat - lat_me)
    valid = jnp.logical_and(row >= -4, row < ROWS + 4)
    code = jnp.where(row < 0, row + ADJ_ROWS, row)
    is_east = dest_lon == (lon_me + 1) % 16
    is_west = dest_lon == (lon_me + 15) % 16
    own_code = jnp.where(jnp.logical_and(valid, dest_lon == lon_me), code.astype(f32), FAR)
    code_t[...] = stacked(own_code).T
    off = jnp.where(is_east, code, jnp.where(is_west, code + ADJ_ROWS, -1))
    side_code[...] = jnp.where(valid, off, -1).astype(f32)
    ends = jnp.concatenate(exact_parts(gathered[pl.ds(32, TILES, stride=40), :]), axis=0).astype(bf16)
    ends = dot(ends, widen[...])
    ends = ends[0:TILES] + ends[TILES : 2 * TILES] + ends[2 * TILES :]
    for c in range(4):
        weights = jnp.zeros((TILES, COLS), f32)
        for w in range(8):
            weights = jnp.where(profile == w, table[c, w], weights)
        prof_t[c] = stacked(weights).T
        for k in range(NFLUX):
            first, final = ends[:, k * COLS : (k + 1) * COLS], ends[:, (4 + k) * COLS : (5 + k) * COLS]
            at = (k * 4 + c) * TILES
            product = weights * jnp.where(is_east, first, final)
            products[0, at : at + TILES, :] = product[:, 0:LANES]
            products[1, at : at + TILES, :] = product[:, LANES:]
    own_matrix(code_t, prof_t, total, high, low)
    return side_sums(products, side_code)


def own_matrix(code_t, prof_t, total, high, low):
    rows = iota((ADJ_ROWS, LANES), 0).astype(f32)

    def build(seg, carry):
        sums = [jnp.zeros((ADJ_ROWS, LANES), f32) for _ in range(4)]
        for r in range(16):
            at = seg * 16 + r
            hit = code_t[pl.ds(at, 1), :] == rows
            for c in range(4):
                sums[c] = sums[c] + jnp.where(hit, prof_t[c, pl.ds(at, 1), :], 0.0)
        for c in range(4):
            total[seg, c] = sums[c]
        return carry

    lax.fori_loop(0, 8, build, 0)
    for seg in range(8):
        whole = total[seg].reshape(4 * ADJ_ROWS, LANES)
        head, tail = split(whole)
        high[:, seg * LANES : (seg + 1) * LANES] = head
        low[:, seg * LANES : (seg + 1) * LANES] = tail


def side_sums(products, side_code):
    bins = iota((2 * ADJ_ROWS, COLS), 0).astype(f32)

    def side(i, sums):
        for j in range(4):
            tile = i * 4 + j
            hit = jnp.where(side_code[pl.ds(tile, 1), :] == bins, 1.0, 0.0).astype(bf16)
            rows = pl.ds(tile, 16, stride=TILES)
            head, tail = split(jnp.concatenate([products[0, rows, :], products[1, rows, :]], axis=1))
            both = jnp.concatenate([head, tail], axis=0)
            sums = sums + lax.dot_general(hit, both, (((1,), (1,)), ((), ())), preferred_element_type=f32)
        return sums

    sums = lax.fori_loop(0, TILES // 4, side, jnp.zeros((2 * ADJ_ROWS, 32), f32))
    return sums[:, 0:16] + sums[:, 16:32]


def spread_tables():
    src, out = np.arange(512)[:, None], np.arange(512)[None, :]
    own = ((src // 64) % 2 == out // COLS) & (out % COLS == 4 * (src % 64) + src // 128)
    src, out = np.arange(LANES)[:, None], np.arange(8 * COLS)[None, :]
    seg = out % COLS // 16
    widen = (src // 16 == out // COLS) & (src % 16 == (seg // 4) * 4 + seg % 4)
    return own.astype(ml_dtypes.bfloat16), widen.astype(ml_dtypes.bfloat16)


def assemble_forcing(gathered, high, low, g_high, g_low, spread_own):
    for seg in range(8):
        for h in range(2):
            s = h * 8 + seg
            at = (s % 4) * 4 + s // 4
            for half in range(2):
                part = gathered[pl.ds(half * 16 + at, TILES, stride=40), :]
                head, tail = split(part)
                rows = slice(seg * LANES + h * 64, seg * LANES + h * 64 + 64)
                g_high[rows, half * LANES : (half + 1) * LANES] = head
                g_low[rows, half * LANES : (half + 1) * LANES] = tail
    coarse = dot(high[...], g_high[...]) + dot(high[...], g_low[...]) + dot(low[...], g_high[...])
    parts = []
    for half in range(2):
        cols = slice(half * LANES, (half + 1) * LANES)
        own = jnp.concatenate([coarse[c * ADJ_ROWS : (c + 1) * ADJ_ROWS, cols] for c in range(4)], axis=1)
        head = own.astype(bf16).astype(f32)
        parts += [head, own - head]
    return dot(jnp.concatenate(parts, axis=0).astype(bf16), spread_own[...])


def forward_steps(state, wet_all, diffusivity, speed_e, speed_n, grad_e, grad_n):
    for step in range(NSTEP):
        now, later = step % 2, (step + 1) % 2
        for l in range(LEVB):
            a = 0.5 * STEP_COEF * (SPEED_BASE + SPEED_GAIN * state[now, l])
            b = (0.5 * STEP_COEF * SPEED_GAIN) * state[now, LEVB + l]
            speed_e[step, l] = to_adjoint_rows(a)
            speed_n[step, l] = to_adjoint_rows(b)
            for f in range(FLD):
                d = diffusivity[f]
                q = state[now, f * LEVB + l]
                q_e, q_w, q_n, q_s = east(q), west(q), north(q), south(q)
                across, along = q_e - q_w, q_n - q_s
                half = -0.5 * STEP_COEF * SPEED_GAIN
                grad_e[step, f, l] = to_adjoint_rows(half * across)
                grad_n[step, f, l] = to_adjoint_rows(half * along)
                if step + 1 < NSTEP:
                    moved = (1.0 - 4.0 * d) * q + d * ((q_e + q_w) + (q_n + q_s)) - a * across - b * along
                    state[later, f * LEVB + l] = wet_all[...] * moved


def ocean_kernel(
    diffusivity_at,
    penetration_at,
    table_at,
    widen_at,
    spread_own_at,
    mask,
    checkpoint,
    adjoint_in,
    from_south,
    from_north,
    from_west,
    from_east,
    gathered,
    out,
    diffusivity,
    penetration,
    table,
    widen,
    spread_own,
    mask_own,
    state,
    lam,
    wet_all,
    wet,
    speed_e,
    speed_n,
    grad_e,
    grad_n,
    high,
    low,
    code_t,
    prof_t,
    total,
    products,
    side_code,
    g_high,
    g_low,
    done,
    sems,
):
    section = lax.axis_index("comp")
    pairs = [
        (diffusivity_at, diffusivity),
        (penetration_at, penetration),
        (table_at, table),
        (widen_at, widen),
        (spread_own_at, spread_own),
        (mask, mask_own),
    ]
    for plane in range(PLANES):
        f, l = plane // LEVB, plane % LEVB
        pairs.append((checkpoint.at[f, l], state.at[0, plane, 0:ROWS, 0:COLS]))
        pairs.append((adjoint_in.at[f, l], lam.at[f, l, 0:ROWS, 0:COLS]))
    copies = [pltpu.make_async_copy(source, target, sems.at[at]) for at, (source, target) in enumerate(pairs)]
    for copy in copies:
        copy.start()

    @pl.when(section == 3)
    def _():
        for copy in copies:
            copy.wait()
        for plane in range(PLANES):
            f, l = plane // LEVB, plane % LEVB
            t = jnp.tanh(state[0, plane, 0:ROWS, 0:COLS])
            done[f, l] = lam[f, l, 0:ROWS, 0:COLS] * (1.0 - t * t)

    @pl.when(section != 3)
    def _():
        for copy in copies[:5]:
            copy.wait()
        sides = route_matrix(gathered, table, widen, high, low, code_t, prof_t, total, products, side_code)
        own = assemble_forcing(gathered, high, low, g_high, g_low, spread_own)

        def edge(start, rows, plane):
            lane = iota((rows, LANES), 1)
            west_side, east_side = from_west[start : start + rows], from_east[start : start + rows]
            if plane:
                east_side = pltpu.roll(east_side, LANES - 8 * plane, 1)
            west_side = pltpu.roll(west_side, (120 - 8 * plane) % LANES, 1)
            return jnp.where(lane < 8, east_side, jnp.where(lane >= 120, west_side, 0.0))

        for f in range(FLD):
            for l in range(LEVB):
                plane = f * LEVB + l
                state[0, plane, ROWS : ROWS + 8, 0:COLS] = from_north[plane]
                state[0, plane, ROWS + 8 :, 0:COLS] = from_south[plane]
                state[0, plane, :, COLS:] = edge(0, HALO_ROWS, plane)
                lam[f, l, ROWS:, 0:COLS] = adjoint_halo(from_north, from_south, f, l)
                lam[f, l, :, COLS:] = edge(HALO_ROWS, ADJ_ROWS, plane)
        at = PLANES + FLD
        for copy in copies[5:]:
            copy.wait()
        wet_all[0:ROWS, 0:COLS] = mask_own[...].astype(f32)
        wet_all[ROWS : ROWS + 8, 0:COLS] = from_north[at]
        wet_all[ROWS + 8 :, 0:COLS] = from_south[at]
        wet_all[:, COLS:] = edge(0, HALO_ROWS, PLANES)
        wet[...] = to_adjoint_rows(wet_all[...])
        lane = iota((ADJ_ROWS, LANES), 1)
        sides = jnp.concatenate([sides, jnp.zeros((2 * ADJ_ROWS, LANES - 16), f32)], axis=1)
        w = wet[...]
        band = lax.axis_index("comp")
        for k in range(NFLUX):
            at, sub = (k // 2) * 2 * ADJ_ROWS, k % 2
            own_k = own[:, sub * COLS : (sub + 1) * COLS]
            own_k = own_k[at : at + ADJ_ROWS] + own_k[at + ADJ_ROWS : at + 2 * ADJ_ROWS]
            first, final = sides[0:ADJ_ROWS], sides[ADJ_ROWS:]
            if k:
                first = pltpu.roll(first, LANES - 4 * k, 1)
            final = pltpu.roll(final, LANES - 4 * k - 4, 1)
            side_k = jnp.where(lane < 4, first, jnp.where(lane >= LANES - 4, final, 0.0))
            forcing = w * jnp.concatenate([own_k, side_k], axis=1)
            for l in range(LEVB):
                lam[k, l] = lam[k, l] + penetration[band * LEVB + l] * forcing

        forward_steps(state, wet_all, diffusivity, speed_e, speed_n, grad_e, grad_n)

        def back(i, carry):
            step = NSTEP - 1 - i
            for l in range(LEVB):
                a, b, w = speed_e[step, l], speed_n[step, l], wet[...]
                sum_e, sum_n = 0.0, 0.0
                for f in (2, 3, 4, 5, 1, 0):
                    mu = w * lam[f, l]
                    sum_e = sum_e + mu * grad_e[step, f, l]
                    sum_n = sum_n + mu * grad_n[step, f, l]
                    lam[f, l] = pulled(mu, a, b, diffusivity[f])
                lam[0, l] = lam[0, l] + sum_e
                lam[1, l] = lam[1, l] + sum_n
            return carry

        lax.fori_loop(0, NSTEP, back, 0)
        for f in range(FLD):
            for l in range(LEVB):
                done[f, l] = lam[f, l, 0:ROWS, 0:COLS]

    copy = pltpu.make_async_copy(done, out, sems.at[0])
    copy.start()
    copy.wait()


def shards(
    checkpoint,
    adjoint_in,
    land_mask,
    diffusivity,
    penetration,
    column_weight,
    routes,
    dest_row,
    weight_id,
    regrid_table,
):
    state, adj = checkpoint[0], adjoint_in[0]
    state_at, adj_at, mask_at = hbm(state), hbm(adj), hbm(land_mask)
    any_place = pl.BlockSpec(memory_space=pl.ANY)
    held = VM((FLD, LEVB, ROWS, COLS), f32)
    edge = shape_of((PLANES + FLD + 1, 8, COLS))
    own_strip = shape_of((2, ROWS, LANES))
    pairs = (2, LANES)
    small = pltpu.CompilerParams(vmem_limit_bytes=2 << 20)
    flux, to_north, to_south, own_east, own_west = pl.pallas_call(
        flux_kernel,
        out_shape=(shape_of((40, LANES)), edge, edge, own_strip, own_strip),
        in_specs=[in_hbm()] * 4,
        out_specs=(vmem(),) * 5,
        scratch_shapes=[
            held,
            held,
            VM((ROWS, COLS), jnp.int32),
            VM((NFLUX, FLD * 32), f32),
            pltpu.SemaphoreType.DMA((4,)),
        ],
        compiler_params=pltpu.CompilerParams(vmem_limit_bytes=12 << 20),
        name="flux",
    )(
        state_at,
        adj_at,
        mask_at,
        hbm(column_weight),
    )
    sent = [lax.ppermute(flux, "comp", [(3, band)]) for band in range(3)]
    rows_up = [(c * 4 + i, c * 4 + i + 1) for c in range(3) for i in range(3)]
    from_south = lax.ppermute(to_north, ("comp", "lat"), rows_up)
    from_north = lax.ppermute(to_south, ("comp", "lat"), [(b, a) for a, b in rows_up])

    payload = pl.pallas_call(
        payload_kernel,
        out_shape=pltpu.HBM((TILES, 40, LANES), f32),
        in_specs=[vmem()] * 4 + [in_hbm()] * 3 + [any_place] * 2,
        out_specs=in_hbm(),
        scratch_shapes=[VM((40, LANES), f32), VM((8, LANES), jnp.int32), pltpu.SemaphoreType.DMA((TILES,))],
        compiler_params=small,
        name="payload",
    )(flux, *sent, *[hbm(x.reshape(pairs)) for x in (routes, dest_row, weight_id)], from_south, from_north)

    strip = shape_of((HALO_ROWS + ADJ_ROWS, LANES))
    to_east, to_west = pl.pallas_call(
        strip_kernel,
        out_shape=(strip, strip),
        in_specs=[vmem()] * 4,
        out_specs=(vmem(),) * 2,
        compiler_params=pltpu.CompilerParams(vmem_limit_bytes=8 << 20),
        name="strips",
    )(own_east, own_west, from_south, from_north)
    cols_up = [(c * 16 + i, c * 16 + (i + 1) % 16) for c in range(3) for i in range(16)]
    from_west = lax.ppermute(to_east, ("comp", "lon"), cols_up)
    from_east = lax.ppermute(to_west, ("comp", "lon"), [(b, a) for a, b in cols_up])

    gathered = lax.all_to_all(payload, ("lat", "lon"), split_axis=0, concat_axis=0, tiled=True)
    gathered = gathered.reshape(TILES * 40, LANES)

    spread_own, widen = spread_tables()
    wide = (ADJ_ROWS, WIDE)
    result = pl.pallas_call(
        ocean_kernel,
        out_shape=pltpu.HBM((FLD, LEVB, ROWS, COLS), f32),
        in_specs=[in_hbm()] * 8 + [vmem()] * 5,
        out_specs=in_hbm(),
        scratch_shapes=[
            SM((FLD,), f32),
            SM((FLD,), f32),
            SM((4, 8), f32),
            VM((LANES, 8 * COLS), bf16),
            VM((512, 512), bf16),
            VM((ROWS, COLS), jnp.int32),
            VM((2, PLANES, HALO_ROWS, WIDE), f32),
            VM((FLD, LEVB) + wide, f32),
            VM((HALO_ROWS, WIDE), f32),
            VM(wide, f32),
            VM((NSTEP, LEVB) + wide, f32),
            VM((NSTEP, LEVB) + wide, f32),
            VM((NSTEP, FLD, LEVB) + wide, f32),
            VM((NSTEP, FLD, LEVB) + wide, f32),
            VM((4 * ADJ_ROWS, 1024), bf16),
            VM((4 * ADJ_ROWS, 1024), bf16),
            VM((LANES, LANES), f32),
            VM((4, LANES, LANES), f32),
            VM((8, 4, ADJ_ROWS, LANES), f32),
            VM((2, 16 * TILES, LANES), f32),
            VM((TILES, COLS), f32),
            VM((1024, COLS), bf16),
            VM((1024, COLS), bf16),
            held,
            pltpu.SemaphoreType.DMA((6 + 2 * PLANES,)),
        ],
        compiler_params=pltpu.CompilerParams(vmem_limit_bytes=48 << 20),
        name="ocean",
    )(
        *[hbm(x) for x in (diffusivity, penetration, regrid_table.T, widen, spread_own)],
        mask_at,
        state_at,
        adj_at,
        from_south,
        from_north,
        from_west,
        from_east,
        gathered,
    )
    return result[None]


def solution(mesh):
    in_specs = (
        P("comp", None, None, "lat", "lon"),
        P("comp", None, None, "lat", "lon"),
        P("lat", "lon"),
        P(),
        P(),
        P(),
        P(("lat", "lon"), None),
        P(("lat", "lon")),
        P(("lat", "lon")),
        P(),
    )
    out_specs = P("comp", None, None, "lat", "lon")
    return jax.shard_map(shards, mesh=mesh, in_specs=in_specs, out_specs=out_specs, check_vma=False)
```

```python
import jax
import jax.numpy as jnp
import ml_dtypes
import numpy as np
from jax import lax
from jax.experimental import pallas as pl
from jax.experimental.pallas import tpu as pltpu
from jax.sharding import PartitionSpec as P

NSTEP = 4
STEP_COEF = 0.2
SPEED_BASE = 0.5
SPEED_GAIN = 0.5

FLD = 6
NFLUX = 4
LEVB = 2
ROWS = 64
COLS = 256
PLANES = FLD * LEVB
HALO_ROWS = 80
ADJ_ROWS = 72
WIDE = 384
LANES = 128
TILES = 64
SEGS = 16
FAR = -1.0

f32 = jnp.float32
bf16 = jnp.bfloat16
VM = pltpu.VMEM
SM = pltpu.SMEM


def vmem():
    return pl.BlockSpec(memory_space=VM)


def smem():
    return pl.BlockSpec(memory_space=SM)


def in_hbm():
    return pl.BlockSpec(memory_space=pltpu.HBM)


def hbm(x):
    return pltpu.with_memory_space_constraint(jnp.asarray(x), pltpu.HBM)


def shape_of(shape, dtype=f32):
    return jax.ShapeDtypeStruct(shape, dtype)


def east(x):
    return pltpu.roll(x, WIDE - 1, 1)


def west(x):
    return pltpu.roll(x, 1, 1)


def north(x):
    return pltpu.roll(x, x.shape[0] - 1, 0)


def south(x):
    return pltpu.roll(x, 1, 0)


def iota(shape, dim):
    return lax.broadcasted_iota(jnp.int32, shape, dim)


def split(x):
    high = x.astype(bf16)
    return high, (x - high.astype(f32)).astype(bf16)


def dot(x, y):
    return jnp.dot(x, y, preferred_element_type=f32)


def exact_parts(x):
    head = x.astype(bf16).astype(f32)
    rest = x - head
    middle = rest.astype(bf16).astype(f32)
    return [head, middle, rest - middle]


def packed_strips(planes_west, planes_east):
    lane_group = iota(planes_west[0].shape, 1) // 8
    east_strip = jnp.zeros(planes_west[0].shape, f32)
    west_strip = east_strip
    for plane, (edge_w, edge_e) in enumerate(zip(planes_west, planes_east)):
        east_strip = jnp.where(lane_group == plane, pltpu.roll(edge_e, 8 * plane + 8, 1), east_strip)
        moved = pltpu.roll(edge_w, 8 * plane, 1) if plane else edge_w
        west_strip = jnp.where(lane_group == plane, moved, west_strip)
    return east_strip, west_strip


def flux_kernel(
    checkpoint,
    adjoint_in,
    mask,
    weight,
    routes,
    dest_row,
    weight_id,
    flux,
    to_north,
    to_south,
    own_east,
    own_west,
    held,
    held_adj,
    held_mask,
    held_weight,
    lists,
    sems,
):
    listing = [
        pltpu.make_async_copy(x, lists.at[pl.ds(2 * at, 2)], sems.at[4 + at])
        for at, x in enumerate((routes, dest_row, weight_id))
    ]
    for copy in listing:
        copy.start()
    flux[40:, :] = jnp.zeros((flux.shape[0] - 40, LANES), f32)
    pairs = ((checkpoint, held), (adjoint_in, held_adj), (mask, held_mask), (weight, held_weight))
    copies = [pltpu.make_async_copy(source, target, sems.at[at]) for at, (source, target) in enumerate(pairs)]
    for copy in copies:
        copy.start()

    @pl.when(lax.axis_index("comp") != 3)
    def _():
        flux[0:33, :] = jnp.zeros((33, LANES), f32)
        for copy in listing:
            copy.wait()
        flux[33:39, :] = lists[0:6, :].astype(f32)
        flux[39:40, :] = jnp.zeros((1, LANES), f32)
        for copy in copies:
            copy.wait()
        top, low = slice(ROWS - 8, ROWS), slice(0, 8)
        row = iota((8, COLS), 0)
        for f in range(FLD):
            for l in range(LEVB):
                to_north[f * LEVB + l] = held[f, l, top, :]
                to_south[f * LEVB + l] = held[f, l, low, :]
            upper = pltpu.roll(held_adj[f, 1, top, :], 4, 0)
            to_north[PLANES + f] = jnp.where(row < 4, upper, held_adj[f, 0, top, :])
            lower = pltpu.roll(held_adj[f, 1, low, :], 4, 0)
            to_south[PLANES + f] = jnp.where(row < 4, held_adj[f, 0, low, :], lower)
        to_north[PLANES + FLD] = held_mask[top, :].astype(f32)
        to_south[PLANES + FLD] = held_mask[low, :].astype(f32)
        for kind, source in enumerate((held, held_adj)):
            planes = [source[plane // LEVB, plane % LEVB] for plane in range(PLANES)]
            if kind == 0:
                planes.append(held_mask[...].astype(f32))
            own_east[kind], own_west[kind] = packed_strips([x[:, 0:LANES] for x in planes], [x[:, LANES:] for x in planes])

    @pl.when(lax.axis_index("comp") == 3)
    def _():
        for copy in listing:
            copy.wait()
        copies[3].wait()
        w = held_weight[...]
        parts = jnp.concatenate(exact_parts(w) + [jnp.zeros_like(w)], axis=0).astype(bf16)
        level, row = iota((FLD * 32, PLANES * ROWS), 0), iota((FLD * 32, PLANES * ROWS), 1)
        repeated = dot(parts, jnp.where(row // 4 == level, 1.0, 0.0).astype(bf16))
        repeated = repeated[0:4] + repeated[4:8] + repeated[8:12]
        own = iota((4, PLANES * ROWS), 1) % 4 == iota((4, PLANES * ROWS), 0)
        spread = jnp.concatenate([jnp.where(own, repeated[k : k + 1], 0.0) for k in range(NFLUX)], axis=0)
        for copy in copies[:3]:
            copy.wait()
        t = jnp.tanh(held[...])
        sens = (held_adj[...] * (1.0 - t * t)).reshape(PLANES * ROWS, COLS)
        by_kind = jnp.dot(spread, sens, precision=lax.Precision.HIGHEST, preferred_element_type=f32)
        rows = []
        for q in range(4):
            rows.append(
                jnp.concatenate(
                    [by_kind[k * 4 : k * 4 + 4, q * 64 : q * 64 + 64] for k in range(NFLUX)], axis=1
                )
            )
        by_seg = jnp.concatenate(rows, axis=0)
        flux[0:16, :] = by_seg[:, 0:LANES]
        flux[16:32, :] = by_seg[:, LANES:]
        lane = iota((COLS, LANES), 1)
        pick = jnp.where(iota((COLS, LANES), 0) == (lane % 4) * 64 + 63 * (lane // 64), 1.0, 0.0).astype(bf16)
        ends = dot(jnp.concatenate(exact_parts(by_kind), axis=0).astype(bf16), pick)
        ends = ends[0:16] + ends[16:32] + ends[32:48]
        lane = iota((16, LANES), 1)
        mine = iota((16, LANES), 0) == (lane // 16 % 4) * 4 + lane // 4 % 4
        flux[32:33, :] = jnp.sum(jnp.where(mine, ends, 0.0), axis=0, keepdims=True)
        flux[33:40, :] = jnp.zeros((7, LANES), f32)


def adjoint_halo(from_north, from_south, f, l):
    high, low = from_north[PLANES + f], from_south[PLANES + f]
    if l:
        high, low = pltpu.roll(high, 4, 0), pltpu.roll(low, 4, 0)
    return jnp.where(iota((8, COLS), 0) < 4, high, low)


def strip_kernel(own_east, own_west, from_south, from_north, to_east, to_west):
    states = [jnp.concatenate([from_north[p], from_south[p]], axis=0) for p in range(PLANES)]
    states.append(jnp.concatenate([from_north[PLANES + FLD], from_south[PLANES + FLD]], axis=0))
    adjoints = [adjoint_halo(from_north, from_south, p // LEVB, p % LEVB) for p in range(PLANES)]
    for target, own in ((to_east, own_east), (to_west, own_west)):
        target[0:ROWS, :] = own[0]
        target[HALO_ROWS : HALO_ROWS + ROWS, :] = own[1]
    for start, planes in ((ROWS, states), (HALO_ROWS + ROWS, adjoints)):
        rows = slice(start, start + planes[0].shape[0])
        to_east[rows, :], to_west[rows, :] = packed_strips([x[:, 0:LANES] for x in planes], [x[:, LANES:] for x in planes])


def payload_kernel(flux, first, second, third, south, north, payload, block, sems):
    del south, north
    block[...] = flux[0:40, :] + (first[0:40, :] + second[0:40, :] + third[0:40, :])
    copies = [pltpu.make_async_copy(block, payload.at[tile], sems.at[tile]) for tile in range(TILES)]
    for copy in copies:
        copy.start()
    for copy in copies:
        copy.wait()


def to_adjoint_rows(x):
    row = iota((8, WIDE), 0)
    return jnp.concatenate([x[0:ROWS], jnp.where(row < 4, x[ROWS : ROWS + 8], x[ROWS + 8 :])], axis=0)


def pulled(mu, a, b, d):
    mixed, carried_e, carried_n = d * mu, a * mu, b * mu
    return (
        (1.0 - 4.0 * d) * mu
        + (east(mixed + carried_e) + west(mixed - carried_e))
        + (north(mixed + carried_n) + south(mixed - carried_n))
    )


def route_matrix(gathered, table, widen, high, low, code_t, prof_t, total, products, side_code):
    lat_me, lon_me = lax.axis_index("lat"), lax.axis_index("lon")

    def listed(at):
        parts = [gathered[pl.ds(33 + 2 * at + half, TILES, stride=40), :] for half in range(2)]
        return jnp.concatenate(parts, axis=1).astype(jnp.int32)

    def stacked(x):
        return jnp.concatenate([x[:, 0:LANES], x[:, LANES:]], axis=0)

    dest, row, profile = listed(0), listed(1), listed(2)
    dest_lat, dest_lon = jnp.right_shift(dest, 4), jnp.bitwise_and(dest, 15)
    row = row + ROWS * (dest_lat - lat_me)
    valid = jnp.logical_and(row >= -4, row < ROWS + 4)
    code = jnp.where(row < 0, row + ADJ_ROWS, row)
    is_east = dest_lon == (lon_me + 1) % 16
    is_west = dest_lon == (lon_me + 15) % 16
    own_code = jnp.where(jnp.logical_and(valid, dest_lon == lon_me), code.astype(f32), FAR)
    code_t[...] = stacked(own_code).T
    off = jnp.where(is_east, code, jnp.where(is_west, code + ADJ_ROWS, -1))
    side_code[...] = jnp.where(valid, off, -1).astype(f32)
    ends = jnp.concatenate(exact_parts(gathered[pl.ds(32, TILES, stride=40), :]), axis=0).astype(bf16)
    ends = dot(ends, widen[...])
    ends = ends[0:TILES] + ends[TILES : 2 * TILES] + ends[2 * TILES :]
    for c in range(4):
        weights = jnp.zeros((TILES, COLS), f32)
        for w in range(8):
            weights = jnp.where(profile == w, table[c, w], weights)
        prof_t[c] = stacked(weights).T
        for k in range(NFLUX):
            first, final = ends[:, k * COLS : (k + 1) * COLS], ends[:, (4 + k) * COLS : (5 + k) * COLS]
            at = (k * 4 + c) * TILES
            product = weights * jnp.where(is_east, first, final)
            products[0, at : at + TILES, :] = product[:, 0:LANES]
            products[1, at : at + TILES, :] = product[:, LANES:]
    own_matrix(code_t, prof_t, total, high, low)
    return side_sums(products, side_code)


def own_matrix(code_t, prof_t, total, high, low):
    rows = iota((ADJ_ROWS, LANES), 0).astype(f32)

    def build(seg, carry):
        sums = [jnp.zeros((ADJ_ROWS, LANES), f32) for _ in range(4)]
        for r in range(16):
            at = seg * 16 + r
            hit = code_t[pl.ds(at, 1), :] == rows
            for c in range(4):
                sums[c] = sums[c] + jnp.where(hit, prof_t[c, pl.ds(at, 1), :], 0.0)
        for c in range(4):
            total[seg, c] = sums[c]
        return carry

    lax.fori_loop(0, 8, build, 0)
    for seg in range(8):
        whole = total[seg].reshape(4 * ADJ_ROWS, LANES)
        head, tail = split(whole)
        high[:, seg * LANES : (seg + 1) * LANES] = head
        low[:, seg * LANES : (seg + 1) * LANES] = tail


def side_sums(products, side_code):
    bins = iota((2 * ADJ_ROWS, COLS), 0).astype(f32)

    def side(i, sums):
        for j in range(4):
            tile = i * 4 + j
            hit = jnp.where(side_code[pl.ds(tile, 1), :] == bins, 1.0, 0.0).astype(bf16)
            rows = pl.ds(tile, 16, stride=TILES)
            head, tail = split(jnp.concatenate([products[0, rows, :], products[1, rows, :]], axis=1))
            both = jnp.concatenate([head, tail], axis=0)
            sums = sums + lax.dot_general(hit, both, (((1,), (1,)), ((), ())), preferred_element_type=f32)
        return sums

    sums = lax.fori_loop(0, TILES // 4, side, jnp.zeros((2 * ADJ_ROWS, 32), f32))
    return sums[:, 0:16] + sums[:, 16:32]


def spread_tables():
    src, out = np.arange(512)[:, None], np.arange(512)[None, :]
    own = ((src // 64) % 2 == out // COLS) & (out % COLS == 4 * (src % 64) + src // 128)
    src, out = np.arange(LANES)[:, None], np.arange(8 * COLS)[None, :]
    seg = out % COLS // 16
    widen = (src // 16 == out // COLS) & (src % 16 == (seg // 4) * 4 + seg % 4)
    return own.astype(ml_dtypes.bfloat16), widen.astype(ml_dtypes.bfloat16)


def assemble_forcing(gathered, high, low, g_high, g_low, spread_own):
    for seg in range(8):
        for h in range(2):
            s = h * 8 + seg
            at = (s % 4) * 4 + s // 4
            for half in range(2):
                part = gathered[pl.ds(half * 16 + at, TILES, stride=40), :]
                head, tail = split(part)
                rows = slice(seg * LANES + h * 64, seg * LANES + h * 64 + 64)
                g_high[rows, half * LANES : (half + 1) * LANES] = head
                g_low[rows, half * LANES : (half + 1) * LANES] = tail
    coarse = dot(high[...], g_high[...]) + dot(high[...], g_low[...]) + dot(low[...], g_high[...])
    parts = []
    for half in range(2):
        cols = slice(half * LANES, (half + 1) * LANES)
        own = jnp.concatenate([coarse[c * ADJ_ROWS : (c + 1) * ADJ_ROWS, cols] for c in range(4)], axis=1)
        head = own.astype(bf16).astype(f32)
        parts += [head, own - head]
    return dot(jnp.concatenate(parts, axis=0).astype(bf16), spread_own[...])


def forward_steps(state, wet_all, diffusivity, speed_e, speed_n, grad_e, grad_n):
    for step in range(NSTEP):
        now, later = step % 2, (step + 1) % 2
        for l in range(LEVB):
            a = 0.5 * STEP_COEF * (SPEED_BASE + SPEED_GAIN * state[now, l])
            b = (0.5 * STEP_COEF * SPEED_GAIN) * state[now, LEVB + l]
            speed_e[step, l] = to_adjoint_rows(a)
            speed_n[step, l] = to_adjoint_rows(b)
            for f in range(FLD):
                d = diffusivity[f]
                q = state[now, f * LEVB + l]
                q_e, q_w, q_n, q_s = east(q), west(q), north(q), south(q)
                across, along = q_e - q_w, q_n - q_s
                half = -0.5 * STEP_COEF * SPEED_GAIN
                grad_e[step, f, l] = to_adjoint_rows(half * across)
                grad_n[step, f, l] = to_adjoint_rows(half * along)
                if step + 1 < NSTEP:
                    moved = (1.0 - 4.0 * d) * q + d * ((q_e + q_w) + (q_n + q_s)) - a * across - b * along
                    state[later, f * LEVB + l] = wet_all[...] * moved


def ocean_kernel(
    diffusivity_at,
    penetration_at,
    table_at,
    widen_at,
    spread_own_at,
    mask,
    checkpoint,
    adjoint_in,
    from_south,
    from_north,
    from_west,
    from_east,
    gathered,
    out,
    diffusivity,
    penetration,
    table,
    widen,
    spread_own,
    mask_own,
    state,
    lam,
    wet_all,
    wet,
    speed_e,
    speed_n,
    grad_e,
    grad_n,
    high,
    low,
    code_t,
    prof_t,
    total,
    products,
    side_code,
    g_high,
    g_low,
    done,
    sems,
):
    section = lax.axis_index("comp")
    pairs = [
        (diffusivity_at, diffusivity),
        (penetration_at, penetration),
        (table_at, table),
        (widen_at, widen),
        (spread_own_at, spread_own),
        (mask, mask_own),
    ]
    for plane in range(PLANES):
        f, l = plane // LEVB, plane % LEVB
        pairs.append((checkpoint.at[f, l], state.at[0, plane, 0:ROWS, 0:COLS]))
        pairs.append((adjoint_in.at[f, l], lam.at[f, l, 0:ROWS, 0:COLS]))
    copies = [pltpu.make_async_copy(source, target, sems.at[at]) for at, (source, target) in enumerate(pairs)]
    for copy in copies:
        copy.start()

    @pl.when(section == 3)
    def _():
        for copy in copies:
            copy.wait()
        for plane in range(PLANES):
            f, l = plane // LEVB, plane % LEVB
            t = jnp.tanh(state[0, plane, 0:ROWS, 0:COLS])
            done[f, l] = lam[f, l, 0:ROWS, 0:COLS] * (1.0 - t * t)

    @pl.when(section != 3)
    def _():
        for copy in copies[:5]:
            copy.wait()
        sides = route_matrix(gathered, table, widen, high, low, code_t, prof_t, total, products, side_code)
        own = assemble_forcing(gathered, high, low, g_high, g_low, spread_own)

        def edge(start, rows, plane):
            lane = iota((rows, LANES), 1)
            west_side, east_side = from_west[start : start + rows], from_east[start : start + rows]
            if plane:
                east_side = pltpu.roll(east_side, LANES - 8 * plane, 1)
            west_side = pltpu.roll(west_side, (120 - 8 * plane) % LANES, 1)
            return jnp.where(lane < 8, east_side, jnp.where(lane >= 120, west_side, 0.0))

        for f in range(FLD):
            for l in range(LEVB):
                plane = f * LEVB + l
                state[0, plane, ROWS : ROWS + 8, 0:COLS] = from_north[plane]
                state[0, plane, ROWS + 8 :, 0:COLS] = from_south[plane]
                state[0, plane, :, COLS:] = edge(0, HALO_ROWS, plane)
                lam[f, l, ROWS:, 0:COLS] = adjoint_halo(from_north, from_south, f, l)
                lam[f, l, :, COLS:] = edge(HALO_ROWS, ADJ_ROWS, plane)
        at = PLANES + FLD
        for copy in copies[5:]:
            copy.wait()
        wet_all[0:ROWS, 0:COLS] = mask_own[...].astype(f32)
        wet_all[ROWS : ROWS + 8, 0:COLS] = from_north[at]
        wet_all[ROWS + 8 :, 0:COLS] = from_south[at]
        wet_all[:, COLS:] = edge(0, HALO_ROWS, PLANES)
        wet[...] = to_adjoint_rows(wet_all[...])
        lane = iota((ADJ_ROWS, LANES), 1)
        sides = jnp.concatenate([sides, jnp.zeros((2 * ADJ_ROWS, LANES - 16), f32)], axis=1)
        w = wet[...]
        band = lax.axis_index("comp")
        for k in range(NFLUX):
            at, sub = (k // 2) * 2 * ADJ_ROWS, k % 2
            own_k = own[:, sub * COLS : (sub + 1) * COLS]
            own_k = own_k[at : at + ADJ_ROWS] + own_k[at + ADJ_ROWS : at + 2 * ADJ_ROWS]
            first, final = sides[0:ADJ_ROWS], sides[ADJ_ROWS:]
            if k:
                first = pltpu.roll(first, LANES - 4 * k, 1)
            final = pltpu.roll(final, LANES - 4 * k - 4, 1)
            side_k = jnp.where(lane < 4, first, jnp.where(lane >= LANES - 4, final, 0.0))
            forcing = w * jnp.concatenate([own_k, side_k], axis=1)
            for l in range(LEVB):
                lam[k, l] = lam[k, l] + penetration[band * LEVB + l] * forcing

        forward_steps(state, wet_all, diffusivity, speed_e, speed_n, grad_e, grad_n)

        def back(i, carry):
            step = NSTEP - 1 - i
            for l in range(LEVB):
                a, b, w = speed_e[step, l], speed_n[step, l], wet[...]
                sum_e, sum_n = 0.0, 0.0
                for f in (2, 3, 4, 5, 1, 0):
                    mu = w * lam[f, l]
                    sum_e = sum_e + mu * grad_e[step, f, l]
                    sum_n = sum_n + mu * grad_n[step, f, l]
                    lam[f, l] = pulled(mu, a, b, diffusivity[f])
                lam[0, l] = lam[0, l] + sum_e
                lam[1, l] = lam[1, l] + sum_n
            return carry

        lax.fori_loop(0, NSTEP, back, 0)
        for f in range(FLD):
            for l in range(LEVB):
                done[f, l] = lam[f, l, 0:ROWS, 0:COLS]

    copy = pltpu.make_async_copy(done, out, sems.at[0])
    copy.start()
    copy.wait()


def shards(
    checkpoint,
    adjoint_in,
    land_mask,
    diffusivity,
    penetration,
    column_weight,
    routes,
    dest_row,
    weight_id,
    regrid_table,
):
    state, adj = checkpoint[0], adjoint_in[0]
    state_at, adj_at, mask_at = hbm(state), hbm(adj), hbm(land_mask)
    any_place = pl.BlockSpec(memory_space=pl.ANY)
    held = VM((FLD, LEVB, ROWS, COLS), f32)
    edge = shape_of((PLANES + FLD + 1, 8, COLS))
    own_strip = shape_of((2, ROWS, LANES))
    pairs = (2, LANES)
    small = pltpu.CompilerParams(vmem_limit_bytes=2 << 20)
    flux, to_north, to_south, own_east, own_west = pl.pallas_call(
        flux_kernel,
        out_shape=(shape_of((312, LANES)), edge, edge, own_strip, own_strip),
        in_specs=[in_hbm()] * 7,
        out_specs=(vmem(),) * 5,
        scratch_shapes=[
            held,
            held,
            VM((ROWS, COLS), jnp.int32),
            VM((NFLUX, FLD * 32), f32),
            VM((8, LANES), jnp.int32),
            pltpu.SemaphoreType.DMA((7,)),
        ],
        compiler_params=pltpu.CompilerParams(vmem_limit_bytes=12 << 20),
        name="flux",
    )(
        state_at,
        adj_at,
        mask_at,
        *[hbm(x) for x in (column_weight, routes.reshape(pairs), dest_row.reshape(pairs), weight_id.reshape(pairs))],
    )
    sent = [lax.ppermute(flux, "comp", [(3, band)]) for band in range(3)]
    rows_up = [(c * 4 + i, c * 4 + i + 1) for c in range(3) for i in range(3)]
    from_south = lax.ppermute(to_north, ("comp", "lat"), rows_up)
    from_north = lax.ppermute(to_south, ("comp", "lat"), [(b, a) for a, b in rows_up])

    payload = pl.pallas_call(
        payload_kernel,
        out_shape=pltpu.HBM((TILES, 40, LANES), f32),
        in_specs=[vmem()] * 4 + [any_place] * 2,
        out_specs=in_hbm(),
        scratch_shapes=[VM((40, LANES), f32), pltpu.SemaphoreType.DMA((TILES,))],
        compiler_params=small,
        name="payload",
    )(flux, *sent, from_south, from_north)

    strip = shape_of((HALO_ROWS + ADJ_ROWS, LANES))
    to_east, to_west = pl.pallas_call(
        strip_kernel,
        out_shape=(strip, strip),
        in_specs=[vmem()] * 4,
        out_specs=(vmem(),) * 2,
        compiler_params=pltpu.CompilerParams(vmem_limit_bytes=8 << 20),
        name="strips",
    )(own_east, own_west, from_south, from_north)
    cols_up = [(c * 16 + i, c * 16 + (i + 1) % 16) for c in range(3) for i in range(16)]
    from_west = lax.ppermute(to_east, ("comp", "lon"), cols_up)
    from_east = lax.ppermute(to_west, ("comp", "lon"), [(b, a) for a, b in cols_up])

    gathered = lax.all_to_all(payload, ("lat", "lon"), split_axis=0, concat_axis=0, tiled=True)
    gathered = gathered.reshape(TILES * 40, LANES)

    spread_own, widen = spread_tables()
    wide = (ADJ_ROWS, WIDE)
    result = pl.pallas_call(
        ocean_kernel,
        out_shape=pltpu.HBM((FLD, LEVB, ROWS, COLS), f32),
        in_specs=[in_hbm()] * 8 + [vmem()] * 5,
        out_specs=in_hbm(),
        scratch_shapes=[
            SM((FLD,), f32),
            SM((FLD,), f32),
            SM((4, 8), f32),
            VM((LANES, 8 * COLS), bf16),
            VM((512, 512), bf16),
            VM((ROWS, COLS), jnp.int32),
            VM((2, PLANES, HALO_ROWS, WIDE), f32),
            VM((FLD, LEVB) + wide, f32),
            VM((HALO_ROWS, WIDE), f32),
            VM(wide, f32),
            VM((NSTEP, LEVB) + wide, f32),
            VM((NSTEP, LEVB) + wide, f32),
            VM((NSTEP, FLD, LEVB) + wide, f32),
            VM((NSTEP, FLD, LEVB) + wide, f32),
            VM((4 * ADJ_ROWS, 1024), bf16),
            VM((4 * ADJ_ROWS, 1024), bf16),
            VM((LANES, LANES), f32),
            VM((4, LANES, LANES), f32),
            VM((8, 4, ADJ_ROWS, LANES), f32),
            VM((2, 16 * TILES, LANES), f32),
            VM((TILES, COLS), f32),
            VM((1024, COLS), bf16),
            VM((1024, COLS), bf16),
            held,
            pltpu.SemaphoreType.DMA((6 + 2 * PLANES,)),
        ],
        compiler_params=pltpu.CompilerParams(vmem_limit_bytes=48 << 20),
        name="ocean",
    )(
        *[hbm(x) for x in (diffusivity, penetration, regrid_table.T, widen, spread_own)],
        mask_at,
        state_at,
        adj_at,
        from_south,
        from_north,
        from_west,
        from_east,
        gathered,
    )
    return result[None]


def solution(mesh):
    in_specs = (
        P("comp", None, None, "lat", "lon"),
        P("comp", None, None, "lat", "lon"),
        P("lat", "lon"),
        P(),
        P(),
        P(),
        P(("lat", "lon"), None),
        P(("lat", "lon")),
        P(("lat", "lon")),
        P(),
    )
    out_specs = P("comp", None, None, "lat", "lon")
    return jax.shard_map(shards, mesh=mesh, in_specs=in_specs, out_specs=out_specs, check_vma=False)
```

```python
import jax
import jax.numpy as jnp
import ml_dtypes
import numpy as np
from jax import lax
from jax.experimental import pallas as pl
from jax.experimental.pallas import tpu as pltpu
from jax.sharding import PartitionSpec as P

NSTEP = 4
STEP_COEF = 0.2
SPEED_BASE = 0.5
SPEED_GAIN = 0.5

FLD = 6
NFLUX = 4
LEVB = 2
ROWS = 64
COLS = 256
PLANES = FLD * LEVB
HALO_ROWS = 80
ADJ_ROWS = 72
WIDE = 384
LANES = 128
TILES = 64
SEGS = 16
FAR = -1.0

f32 = jnp.float32
bf16 = jnp.bfloat16
VM = pltpu.VMEM
SM = pltpu.SMEM


def vmem():
    return pl.BlockSpec(memory_space=VM)


def smem():
    return pl.BlockSpec(memory_space=SM)


def in_hbm():
    return pl.BlockSpec(memory_space=pltpu.HBM)


def hbm(x):
    return pltpu.with_memory_space_constraint(jnp.asarray(x), pltpu.HBM)


def shape_of(shape, dtype=f32):
    return jax.ShapeDtypeStruct(shape, dtype)


def east(x):
    return pltpu.roll(x, WIDE - 1, 1)


def west(x):
    return pltpu.roll(x, 1, 1)


def north(x):
    return pltpu.roll(x, x.shape[0] - 1, 0)


def south(x):
    return pltpu.roll(x, 1, 0)


def iota(shape, dim):
    return lax.broadcasted_iota(jnp.int32, shape, dim)


def split(x):
    high = x.astype(bf16)
    return high, (x - high.astype(f32)).astype(bf16)


def dot(x, y):
    return jnp.dot(x, y, preferred_element_type=f32)


def exact_parts(x):
    head = x.astype(bf16).astype(f32)
    rest = x - head
    middle = rest.astype(bf16).astype(f32)
    return [head, middle, rest - middle]


def packed_strips(planes_west, planes_east):
    lane_group = iota(planes_west[0].shape, 1) // 8
    east_strip = jnp.zeros(planes_west[0].shape, f32)
    west_strip = east_strip
    for plane, (edge_w, edge_e) in enumerate(zip(planes_west, planes_east)):
        east_strip = jnp.where(lane_group == plane, pltpu.roll(edge_e, 8 * plane + 8, 1), east_strip)
        moved = pltpu.roll(edge_w, 8 * plane, 1) if plane else edge_w
        west_strip = jnp.where(lane_group == plane, moved, west_strip)
    return east_strip, west_strip


def flux_kernel(
    checkpoint,
    adjoint_in,
    mask,
    weight,
    routes,
    dest_row,
    weight_id,
    flux,
    to_north,
    to_south,
    own_east,
    own_west,
    held,
    held_adj,
    held_mask,
    held_weight,
    lists,
    sems,
):
    listing = [
        pltpu.make_async_copy(x, lists.at[pl.ds(2 * at, 2)], sems.at[4 + at])
        for at, x in enumerate((routes, dest_row, weight_id))
    ]
    for copy in listing:
        copy.start()
    pairs = ((checkpoint, held), (adjoint_in, held_adj), (mask, held_mask), (weight, held_weight))
    copies = [pltpu.make_async_copy(source, target, sems.at[at]) for at, (source, target) in enumerate(pairs)]
    for copy in copies:
        copy.start()

    @pl.when(lax.axis_index("comp") != 3)
    def _():
        flux[0:33, :] = jnp.zeros((33, LANES), f32)
        for copy in listing:
            copy.wait()
        flux[33:39, :] = lists[0:6, :].astype(f32)
        flux[39:40, :] = jnp.zeros((1, LANES), f32)
        for copy in copies:
            copy.wait()
        top, low = slice(ROWS - 8, ROWS), slice(0, 8)
        row = iota((8, COLS), 0)
        for f in range(FLD):
            for l in range(LEVB):
                to_north[f * LEVB + l] = held[f, l, top, :]
                to_south[f * LEVB + l] = held[f, l, low, :]
            upper = pltpu.roll(held_adj[f, 1, top, :], 4, 0)
            to_north[PLANES + f] = jnp.where(row < 4, upper, held_adj[f, 0, top, :])
            lower = pltpu.roll(held_adj[f, 1, low, :], 4, 0)
            to_south[PLANES + f] = jnp.where(row < 4, held_adj[f, 0, low, :], lower)
        to_north[PLANES + FLD] = held_mask[top, :].astype(f32)
        to_south[PLANES + FLD] = held_mask[low, :].astype(f32)
        for kind, source in enumerate((held, held_adj)):
            planes = [source[plane // LEVB, plane % LEVB] for plane in range(PLANES)]
            if kind == 0:
                planes.append(held_mask[...].astype(f32))
            own_east[kind], own_west[kind] = packed_strips([x[:, 0:LANES] for x in planes], [x[:, LANES:] for x in planes])

    @pl.when(lax.axis_index("comp") == 3)
    def _():
        for copy in listing:
            copy.wait()
        copies[3].wait()
        w = held_weight[...]
        parts = jnp.concatenate(exact_parts(w) + [jnp.zeros_like(w)], axis=0).astype(bf16)
        level, row = iota((FLD * 32, PLANES * ROWS), 0), iota((FLD * 32, PLANES * ROWS), 1)
        repeated = dot(parts, jnp.where(row // 4 == level, 1.0, 0.0).astype(bf16))
        repeated = repeated[0:4] + repeated[4:8] + repeated[8:12]
        own = iota((4, PLANES * ROWS), 1) % 4 == iota((4, PLANES * ROWS), 0)
        spread = jnp.concatenate([jnp.where(own, repeated[k : k + 1], 0.0) for k in range(NFLUX)], axis=0)
        for copy in copies[:3]:
            copy.wait()
        t = jnp.tanh(held[...])
        sens = (held_adj[...] * (1.0 - t * t)).reshape(PLANES * ROWS, COLS)
        by_kind = jnp.dot(spread, sens, precision=lax.Precision.HIGHEST, preferred_element_type=f32)
        rows = []
        for q in range(4):
            rows.append(
                jnp.concatenate(
                    [by_kind[k * 4 : k * 4 + 4, q * 64 : q * 64 + 64] for k in range(NFLUX)], axis=1
                )
            )
        by_seg = jnp.concatenate(rows, axis=0)
        flux[0:16, :] = by_seg[:, 0:LANES]
        flux[16:32, :] = by_seg[:, LANES:]
        lane = iota((COLS, LANES), 1)
        pick = jnp.where(iota((COLS, LANES), 0) == (lane % 4) * 64 + 63 * (lane // 64), 1.0, 0.0).astype(bf16)
        ends = dot(jnp.concatenate(exact_parts(by_kind), axis=0).astype(bf16), pick)
        ends = ends[0:16] + ends[16:32] + ends[32:48]
        lane = iota((16, LANES), 1)
        mine = iota((16, LANES), 0) == (lane // 16 % 4) * 4 + lane // 4 % 4
        flux[32:33, :] = jnp.sum(jnp.where(mine, ends, 0.0), axis=0, keepdims=True)
        flux[33:40, :] = jnp.zeros((7, LANES), f32)


def adjoint_halo(from_north, from_south, f, l):
    high, low = from_north[PLANES + f], from_south[PLANES + f]
    if l:
        high, low = pltpu.roll(high, 4, 0), pltpu.roll(low, 4, 0)
    return jnp.where(iota((8, COLS), 0) < 4, high, low)


def strip_kernel(own_east, own_west, from_south, from_north, to_east, to_west):
    states = [jnp.concatenate([from_north[p], from_south[p]], axis=0) for p in range(PLANES)]
    states.append(jnp.concatenate([from_north[PLANES + FLD], from_south[PLANES + FLD]], axis=0))
    adjoints = [adjoint_halo(from_north, from_south, p // LEVB, p % LEVB) for p in range(PLANES)]
    for target, own in ((to_east, own_east), (to_west, own_west)):
        target[0:ROWS, :] = own[0]
        target[HALO_ROWS : HALO_ROWS + ROWS, :] = own[1]
    for start, planes in ((ROWS, states), (HALO_ROWS + ROWS, adjoints)):
        rows = slice(start, start + planes[0].shape[0])
        to_east[rows, :], to_west[rows, :] = packed_strips([x[:, 0:LANES] for x in planes], [x[:, LANES:] for x in planes])


def payload_kernel(flux, first, second, third, south, north, payload, block, sems):
    del south, north
    block[...] = flux[0:40, :] + (first[0:40, :] + second[0:40, :] + third[0:40, :])
    copies = [pltpu.make_async_copy(block, payload.at[tile], sems.at[tile]) for tile in range(TILES)]
    for copy in copies:
        copy.start()
    for copy in copies:
        copy.wait()


def to_adjoint_rows(x):
    row = iota((8, WIDE), 0)
    return jnp.concatenate([x[0:ROWS], jnp.where(row < 4, x[ROWS : ROWS + 8], x[ROWS + 8 :])], axis=0)


def pulled(mu, a, b, d):
    mixed, carried_e, carried_n = d * mu, a * mu, b * mu
    return (
        (1.0 - 4.0 * d) * mu
        + (east(mixed + carried_e) + west(mixed - carried_e))
        + (north(mixed + carried_n) + south(mixed - carried_n))
    )


def route_matrix(gathered, table, widen, high, low, code_t, prof_t, total, products, side_code):
    lat_me, lon_me = lax.axis_index("lat"), lax.axis_index("lon")

    def listed(at):
        parts = [gathered[pl.ds(33 + 2 * at + half, TILES, stride=40), :] for half in range(2)]
        return jnp.concatenate(parts, axis=1).astype(jnp.int32)

    def stacked(x):
        return jnp.concatenate([x[:, 0:LANES], x[:, LANES:]], axis=0)

    dest, row, profile = listed(0), listed(1), listed(2)
    dest_lat, dest_lon = jnp.right_shift(dest, 4), jnp.bitwise_and(dest, 15)
    row = row + ROWS * (dest_lat - lat_me)
    valid = jnp.logical_and(row >= -4, row < ROWS + 4)
    code = jnp.where(row < 0, row + ADJ_ROWS, row)
    is_east = dest_lon == (lon_me + 1) % 16
    is_west = dest_lon == (lon_me + 15) % 16
    own_code = jnp.where(jnp.logical_and(valid, dest_lon == lon_me), code.astype(f32), FAR)
    code_t[...] = stacked(own_code).T
    off = jnp.where(is_east, code, jnp.where(is_west, code + ADJ_ROWS, -1))
    side_code[...] = jnp.where(valid, off, -1).astype(f32)
    ends = jnp.concatenate(exact_parts(gathered[pl.ds(32, TILES, stride=40), :]), axis=0).astype(bf16)
    ends = dot(ends, widen[...])
    ends = ends[0:TILES] + ends[TILES : 2 * TILES] + ends[2 * TILES :]
    for c in range(4):
        weights = jnp.zeros((TILES, COLS), f32)
        for w in range(8):
            weights = jnp.where(profile == w, table[c, w], weights)
        prof_t[c] = stacked(weights).T
        for k in range(NFLUX):
            first, final = ends[:, k * COLS : (k + 1) * COLS], ends[:, (4 + k) * COLS : (5 + k) * COLS]
            at = (k * 4 + c) * TILES
            product = weights * jnp.where(is_east, first, final)
            products[0, at : at + TILES, :] = product[:, 0:LANES]
            products[1, at : at + TILES, :] = product[:, LANES:]
    own_matrix(code_t, prof_t, total, high, low)
    return side_sums(products, side_code)


def own_matrix(code_t, prof_t, total, high, low):
    rows = iota((ADJ_ROWS, LANES), 0).astype(f32)

    def build(seg, carry):
        sums = [jnp.zeros((ADJ_ROWS, LANES), f32) for _ in range(4)]
        for r in range(16):
            at = seg * 16 + r
            hit = code_t[pl.ds(at, 1), :] == rows
            for c in range(4):
                sums[c] = sums[c] + jnp.where(hit, prof_t[c, pl.ds(at, 1), :], 0.0)
        for c in range(4):
            total[seg, c] = sums[c]
        return carry

    lax.fori_loop(0, 8, build, 0)
    for seg in range(8):
        whole = total[seg].reshape(4 * ADJ_ROWS, LANES)
        head, tail = split(whole)
        high[:, seg * LANES : (seg + 1) * LANES] = head
        low[:, seg * LANES : (seg + 1) * LANES] = tail


def side_sums(products, side_code):
    bins = iota((2 * ADJ_ROWS, COLS), 0).astype(f32)

    def side(i, sums):
        for j in range(4):
            tile = i * 4 + j
            hit = jnp.where(side_code[pl.ds(tile, 1), :] == bins, 1.0, 0.0).astype(bf16)
            rows = pl.ds(tile, 16, stride=TILES)
            head, tail = split(jnp.concatenate([products[0, rows, :], products[1, rows, :]], axis=1))
            both = jnp.concatenate([head, tail], axis=0)
            sums = sums + lax.dot_general(hit, both, (((1,), (1,)), ((), ())), preferred_element_type=f32)
        return sums

    sums = lax.fori_loop(0, TILES // 4, side, jnp.zeros((2 * ADJ_ROWS, 32), f32))
    return sums[:, 0:16] + sums[:, 16:32]


def spread_tables():
    src, out = np.arange(512)[:, None], np.arange(512)[None, :]
    own = ((src // 64) % 2 == out // COLS) & (out % COLS == 4 * (src % 64) + src // 128)
    src, out = np.arange(LANES)[:, None], np.arange(8 * COLS)[None, :]
    seg = out % COLS // 16
    widen = (src // 16 == out // COLS) & (src % 16 == (seg // 4) * 4 + seg % 4)
    return own.astype(ml_dtypes.bfloat16), widen.astype(ml_dtypes.bfloat16)


def assemble_forcing(gathered, high, low, g_high, g_low, spread_own):
    for seg in range(8):
        for h in range(2):
            s = h * 8 + seg
            at = (s % 4) * 4 + s // 4
            for half in range(2):
                part = gathered[pl.ds(half * 16 + at, TILES, stride=40), :]
                head, tail = split(part)
                rows = slice(seg * LANES + h * 64, seg * LANES + h * 64 + 64)
                g_high[rows, half * LANES : (half + 1) * LANES] = head
                g_low[rows, half * LANES : (half + 1) * LANES] = tail
    coarse = dot(high[...], g_high[...]) + dot(high[...], g_low[...]) + dot(low[...], g_high[...])
    parts = []
    for half in range(2):
        cols = slice(half * LANES, (half + 1) * LANES)
        own = jnp.concatenate([coarse[c * ADJ_ROWS : (c + 1) * ADJ_ROWS, cols] for c in range(4)], axis=1)
        head = own.astype(bf16).astype(f32)
        parts += [head, own - head]
    return dot(jnp.concatenate(parts, axis=0).astype(bf16), spread_own[...])


def forward_steps(state, wet_all, diffusivity, speed_e, speed_n, grad_e, grad_n):
    for step in range(NSTEP):
        now, later = step % 2, (step + 1) % 2
        for l in range(LEVB):
            a = 0.5 * STEP_COEF * (SPEED_BASE + SPEED_GAIN * state[now, l])
            b = (0.5 * STEP_COEF * SPEED_GAIN) * state[now, LEVB + l]
            speed_e[step, l] = to_adjoint_rows(a)
            speed_n[step, l] = to_adjoint_rows(b)
            for f in range(FLD):
                d = diffusivity[f]
                q = state[now, f * LEVB + l]
                q_e, q_w, q_n, q_s = east(q), west(q), north(q), south(q)
                across, along = q_e - q_w, q_n - q_s
                half = -0.5 * STEP_COEF * SPEED_GAIN
                grad_e[step, f, l] = to_adjoint_rows(half * across)
                grad_n[step, f, l] = to_adjoint_rows(half * along)
                if step + 1 < NSTEP:
                    moved = (1.0 - 4.0 * d) * q + d * ((q_e + q_w) + (q_n + q_s)) - a * across - b * along
                    state[later, f * LEVB + l] = wet_all[...] * moved


def ocean_kernel(
    diffusivity_at,
    penetration_at,
    table_at,
    widen_at,
    spread_own_at,
    mask,
    checkpoint,
    adjoint_in,
    from_south,
    from_north,
    from_west,
    from_east,
    gathered,
    out,
    diffusivity,
    penetration,
    table,
    widen,
    spread_own,
    mask_own,
    state,
    lam,
    wet_all,
    wet,
    speed_e,
    speed_n,
    grad_e,
    grad_n,
    high,
    low,
    code_t,
    prof_t,
    total,
    products,
    side_code,
    g_high,
    g_low,
    done,
    sems,
):
    section = lax.axis_index("comp")
    pairs = [
        (diffusivity_at, diffusivity),
        (penetration_at, penetration),
        (table_at, table),
        (widen_at, widen),
        (spread_own_at, spread_own),
        (mask, mask_own),
    ]
    for plane in range(PLANES):
        f, l = plane // LEVB, plane % LEVB
        pairs.append((checkpoint.at[f, l], state.at[0, plane, 0:ROWS, 0:COLS]))
        pairs.append((adjoint_in.at[f, l], lam.at[f, l, 0:ROWS, 0:COLS]))
    copies = [pltpu.make_async_copy(source, target, sems.at[at]) for at, (source, target) in enumerate(pairs)]
    for copy in copies:
        copy.start()

    @pl.when(section == 3)
    def _():
        for copy in copies:
            copy.wait()
        for plane in range(PLANES):
            f, l = plane // LEVB, plane % LEVB
            t = jnp.tanh(state[0, plane, 0:ROWS, 0:COLS])
            done[f, l] = lam[f, l, 0:ROWS, 0:COLS] * (1.0 - t * t)

    @pl.when(section != 3)
    def _():
        for copy in copies[:5]:
            copy.wait()
        sides = route_matrix(gathered, table, widen, high, low, code_t, prof_t, total, products, side_code)
        own = assemble_forcing(gathered, high, low, g_high, g_low, spread_own)

        def edge(start, rows, plane):
            lane = iota((rows, LANES), 1)
            west_side, east_side = from_west[start : start + rows], from_east[start : start + rows]
            if plane:
                east_side = pltpu.roll(east_side, LANES - 8 * plane, 1)
            west_side = pltpu.roll(west_side, (120 - 8 * plane) % LANES, 1)
            return jnp.where(lane < 8, east_side, jnp.where(lane >= 120, west_side, 0.0))

        for f in range(FLD):
            for l in range(LEVB):
                plane = f * LEVB + l
                state[0, plane, ROWS : ROWS + 8, 0:COLS] = from_north[plane]
                state[0, plane, ROWS + 8 :, 0:COLS] = from_south[plane]
                state[0, plane, :, COLS:] = edge(0, HALO_ROWS, plane)
                lam[f, l, ROWS:, 0:COLS] = adjoint_halo(from_north, from_south, f, l)
                lam[f, l, :, COLS:] = edge(HALO_ROWS, ADJ_ROWS, plane)
        at = PLANES + FLD
        for copy in copies[5:]:
            copy.wait()
        wet_all[0:ROWS, 0:COLS] = mask_own[...].astype(f32)
        wet_all[ROWS : ROWS + 8, 0:COLS] = from_north[at]
        wet_all[ROWS + 8 :, 0:COLS] = from_south[at]
        wet_all[:, COLS:] = edge(0, HALO_ROWS, PLANES)
        wet[...] = to_adjoint_rows(wet_all[...])
        lane = iota((ADJ_ROWS, LANES), 1)
        sides = jnp.concatenate([sides, jnp.zeros((2 * ADJ_ROWS, LANES - 16), f32)], axis=1)
        w = wet[...]
        band = lax.axis_index("comp")
        for k in range(NFLUX):
            at, sub = (k // 2) * 2 * ADJ_ROWS, k % 2
            own_k = own[:, sub * COLS : (sub + 1) * COLS]
            own_k = own_k[at : at + ADJ_ROWS] + own_k[at + ADJ_ROWS : at + 2 * ADJ_ROWS]
            first, final = sides[0:ADJ_ROWS], sides[ADJ_ROWS:]
            if k:
                first = pltpu.roll(first, LANES - 4 * k, 1)
            final = pltpu.roll(final, LANES - 4 * k - 4, 1)
            side_k = jnp.where(lane < 4, first, jnp.where(lane >= LANES - 4, final, 0.0))
            forcing = w * jnp.concatenate([own_k, side_k], axis=1)
            for l in range(LEVB):
                lam[k, l] = lam[k, l] + penetration[band * LEVB + l] * forcing

        forward_steps(state, wet_all, diffusivity, speed_e, speed_n, grad_e, grad_n)

        def back(i, carry):
            step = NSTEP - 1 - i
            for l in range(LEVB):
                a, b, w = speed_e[step, l], speed_n[step, l], wet[...]
                sum_e, sum_n = 0.0, 0.0
                for f in (2, 3, 4, 5, 1, 0):
                    mu = w * lam[f, l]
                    sum_e = sum_e + mu * grad_e[step, f, l]
                    sum_n = sum_n + mu * grad_n[step, f, l]
                    lam[f, l] = pulled(mu, a, b, diffusivity[f])
                lam[0, l] = lam[0, l] + sum_e
                lam[1, l] = lam[1, l] + sum_n
            return carry

        lax.fori_loop(0, NSTEP, back, 0)
        for f in range(FLD):
            for l in range(LEVB):
                done[f, l] = lam[f, l, 0:ROWS, 0:COLS]

    copy = pltpu.make_async_copy(done, out, sems.at[0])
    copy.start()
    copy.wait()


def shards(
    checkpoint,
    adjoint_in,
    land_mask,
    diffusivity,
    penetration,
    column_weight,
    routes,
    dest_row,
    weight_id,
    regrid_table,
):
    state, adj = checkpoint[0], adjoint_in[0]
    state_at, adj_at, mask_at = hbm(state), hbm(adj), hbm(land_mask)
    any_place = pl.BlockSpec(memory_space=pl.ANY)
    held = VM((FLD, LEVB, ROWS, COLS), f32)
    edge = shape_of((PLANES + FLD + 1, 8, COLS))
    own_strip = shape_of((2, ROWS, LANES))
    pairs = (2, LANES)
    small = pltpu.CompilerParams(vmem_limit_bytes=2 << 20)
    flux, to_north, to_south, own_east, own_west = pl.pallas_call(
        flux_kernel,
        out_shape=(shape_of((40, LANES)), edge, edge, own_strip, own_strip),
        in_specs=[in_hbm()] * 7,
        out_specs=(vmem(),) * 5,
        scratch_shapes=[
            held,
            held,
            VM((ROWS, COLS), jnp.int32),
            VM((NFLUX, FLD * 32), f32),
            VM((8, LANES), jnp.int32),
            pltpu.SemaphoreType.DMA((7,)),
        ],
        compiler_params=pltpu.CompilerParams(vmem_limit_bytes=12 << 20),
        name="flux",
    )(
        state_at,
        adj_at,
        mask_at,
        *[hbm(x) for x in (column_weight, routes.reshape(pairs), dest_row.reshape(pairs), weight_id.reshape(pairs))],
    )
    sent = [lax.ppermute(flux, "comp", [(3, band)]) for band in (1, 0, 2)]
    rows_up = [(c * 4 + i, c * 4 + i + 1) for c in range(3) for i in range(3)]
    from_south = lax.ppermute(to_north, ("comp", "lat"), rows_up)
    from_north = lax.ppermute(to_south, ("comp", "lat"), [(b, a) for a, b in rows_up])

    payload = pl.pallas_call(
        payload_kernel,
        out_shape=pltpu.HBM((TILES, 40, LANES), f32),
        in_specs=[vmem()] * 4 + [any_place] * 2,
        out_specs=in_hbm(),
        scratch_shapes=[VM((40, LANES), f32), pltpu.SemaphoreType.DMA((TILES,))],
        compiler_params=small,
        name="payload",
    )(flux, *sent, from_south, from_north)

    strip = shape_of((HALO_ROWS + ADJ_ROWS, LANES))
    to_east, to_west = pl.pallas_call(
        strip_kernel,
        out_shape=(strip, strip),
        in_specs=[vmem()] * 4,
        out_specs=(vmem(),) * 2,
        compiler_params=pltpu.CompilerParams(vmem_limit_bytes=8 << 20),
        name="strips",
    )(own_east, own_west, from_south, from_north)
    cols_up = [(c * 16 + i, c * 16 + (i + 1) % 16) for c in range(3) for i in range(16)]
    from_west = lax.ppermute(to_east, ("comp", "lon"), cols_up)
    from_east = lax.ppermute(to_west, ("comp", "lon"), [(b, a) for a, b in cols_up])

    gathered = lax.all_to_all(payload, ("lat", "lon"), split_axis=0, concat_axis=0, tiled=True)
    gathered = gathered.reshape(TILES * 40, LANES)

    spread_own, widen = spread_tables()
    wide = (ADJ_ROWS, WIDE)
    result = pl.pallas_call(
        ocean_kernel,
        out_shape=pltpu.HBM((FLD, LEVB, ROWS, COLS), f32),
        in_specs=[in_hbm()] * 8 + [vmem()] * 5,
        out_specs=in_hbm(),
        scratch_shapes=[
            SM((FLD,), f32),
            SM((FLD,), f32),
            SM((4, 8), f32),
            VM((LANES, 8 * COLS), bf16),
            VM((512, 512), bf16),
            VM((ROWS, COLS), jnp.int32),
            VM((2, PLANES, HALO_ROWS, WIDE), f32),
            VM((FLD, LEVB) + wide, f32),
            VM((HALO_ROWS, WIDE), f32),
            VM(wide, f32),
            VM((NSTEP, LEVB) + wide, f32),
            VM((NSTEP, LEVB) + wide, f32),
            VM((NSTEP, FLD, LEVB) + wide, f32),
            VM((NSTEP, FLD, LEVB) + wide, f32),
            VM((4 * ADJ_ROWS, 1024), bf16),
            VM((4 * ADJ_ROWS, 1024), bf16),
            VM((LANES, LANES), f32),
            VM((4, LANES, LANES), f32),
            VM((8, 4, ADJ_ROWS, LANES), f32),
            VM((2, 16 * TILES, LANES), f32),
            VM((TILES, COLS), f32),
            VM((1024, COLS), bf16),
            VM((1024, COLS), bf16),
            held,
            pltpu.SemaphoreType.DMA((6 + 2 * PLANES,)),
        ],
        compiler_params=pltpu.CompilerParams(vmem_limit_bytes=48 << 20),
        name="ocean",
    )(
        *[hbm(x) for x in (diffusivity, penetration, regrid_table.T, widen, spread_own)],
        mask_at,
        state_at,
        adj_at,
        from_south,
        from_north,
        from_west,
        from_east,
        gathered,
    )
    return result[None]


def solution(mesh):
    in_specs = (
        P("comp", None, None, "lat", "lon"),
        P("comp", None, None, "lat", "lon"),
        P("lat", "lon"),
        P(),
        P(),
        P(),
        P(("lat", "lon"), None),
        P(("lat", "lon")),
        P(("lat", "lon")),
        P(),
    )
    out_specs = P("comp", None, None, "lat", "lon")
    return jax.shard_map(shards, mesh=mesh, in_specs=in_specs, out_specs=out_specs, check_vma=False)
```

```python
import jax
import jax.numpy as jnp
import ml_dtypes
import numpy as np
from jax import lax
from jax.experimental import pallas as pl
from jax.experimental.pallas import tpu as pltpu
from jax.sharding import PartitionSpec as P

NSTEP = 4
STEP_COEF = 0.2
SPEED_BASE = 0.5
SPEED_GAIN = 0.5

FLD = 6
NFLUX = 4
LEVB = 2
ROWS = 64
COLS = 256
PLANES = FLD * LEVB
HALO_ROWS = 80
ADJ_ROWS = 72
WIDE = 384
LANES = 128
TILES = 64
SEGS = 16
FAR = -1.0

f32 = jnp.float32
bf16 = jnp.bfloat16
VM = pltpu.VMEM
SM = pltpu.SMEM


def vmem():
    return pl.BlockSpec(memory_space=VM)


def smem():
    return pl.BlockSpec(memory_space=SM)


def in_hbm():
    return pl.BlockSpec(memory_space=pltpu.HBM)


def hbm(x):
    return pltpu.with_memory_space_constraint(jnp.asarray(x), pltpu.HBM)


def shape_of(shape, dtype=f32):
    return jax.ShapeDtypeStruct(shape, dtype)


def east(x):
    return pltpu.roll(x, WIDE - 1, 1)


def west(x):
    return pltpu.roll(x, 1, 1)


def north(x):
    return pltpu.roll(x, x.shape[0] - 1, 0)


def south(x):
    return pltpu.roll(x, 1, 0)


def iota(shape, dim):
    return lax.broadcasted_iota(jnp.int32, shape, dim)


def split(x):
    high = x.astype(bf16)
    return high, (x - high.astype(f32)).astype(bf16)


def dot(x, y):
    return jnp.dot(x, y, preferred_element_type=f32)


def exact_parts(x):
    head = x.astype(bf16).astype(f32)
    rest = x - head
    middle = rest.astype(bf16).astype(f32)
    return [head, middle, rest - middle]


def packed_strips(planes_west, planes_east):
    lane_group = iota(planes_west[0].shape, 1) // 8
    east_strip = jnp.zeros(planes_west[0].shape, f32)
    west_strip = east_strip
    for plane, (edge_w, edge_e) in enumerate(zip(planes_west, planes_east)):
        east_strip = jnp.where(lane_group == plane, pltpu.roll(edge_e, 8 * plane + 8, 1), east_strip)
        moved = pltpu.roll(edge_w, 8 * plane, 1) if plane else edge_w
        west_strip = jnp.where(lane_group == plane, moved, west_strip)
    return east_strip, west_strip


def flux_kernel(
    checkpoint,
    adjoint_in,
    mask,
    weight,
    routes,
    dest_row,
    weight_id,
    flux,
    to_north,
    to_south,
    own_east,
    own_west,
    held,
    held_adj,
    held_mask,
    held_weight,
    lists,
    sems,
):
    listing = [
        pltpu.make_async_copy(x, lists.at[pl.ds(2 * at, 2)], sems.at[4 + at])
        for at, x in enumerate((routes, dest_row, weight_id))
    ]
    for copy in listing:
        copy.start()
    pairs = ((checkpoint, held), (adjoint_in, held_adj), (mask, held_mask), (weight, held_weight))
    copies = [pltpu.make_async_copy(source, target, sems.at[at]) for at, (source, target) in enumerate(pairs)]
    for copy in copies:
        copy.start()

    @pl.when(lax.axis_index("comp") != 3)
    def _():
        flux[0:33, :] = jnp.zeros((33, LANES), f32)
        for copy in listing:
            copy.wait()
        flux[33:39, :] = lists[0:6, :].astype(f32)
        flux[39:40, :] = jnp.zeros((1, LANES), f32)
        for copy in copies:
            copy.wait()
        top, low = slice(ROWS - 8, ROWS), slice(0, 8)
        row = iota((8, COLS), 0)
        for f in range(FLD):
            for l in range(LEVB):
                to_north[f * LEVB + l] = held[f, l, top, :]
                to_south[f * LEVB + l] = held[f, l, low, :]
            upper = pltpu.roll(held_adj[f, 1, top, :], 4, 0)
            to_north[PLANES + f] = jnp.where(row < 4, upper, held_adj[f, 0, top, :])
            lower = pltpu.roll(held_adj[f, 1, low, :], 4, 0)
            to_south[PLANES + f] = jnp.where(row < 4, held_adj[f, 0, low, :], lower)
        to_north[PLANES + FLD] = held_mask[top, :].astype(f32)
        to_south[PLANES + FLD] = held_mask[low, :].astype(f32)
        for kind, source in enumerate((held, held_adj)):
            planes = [source[plane // LEVB, plane % LEVB] for plane in range(PLANES)]
            if kind == 0:
                planes.append(held_mask[...].astype(f32))
            own_east[kind], own_west[kind] = packed_strips([x[:, 0:LANES] for x in planes], [x[:, LANES:] for x in planes])

    @pl.when(lax.axis_index("comp") == 3)
    def _():
        for copy in listing:
            copy.wait()
        copies[3].wait()
        w = held_weight[...]
        parts = jnp.concatenate(exact_parts(w) + [jnp.zeros_like(w)], axis=0).astype(bf16)
        level, row = iota((FLD * 32, PLANES * ROWS), 0), iota((FLD * 32, PLANES * ROWS), 1)
        repeated = dot(parts, jnp.where(row // 4 == level, 1.0, 0.0).astype(bf16))
        repeated = repeated[0:4] + repeated[4:8] + repeated[8:12]
        own = iota((4, PLANES * ROWS), 1) % 4 == iota((4, PLANES * ROWS), 0)
        spread = jnp.concatenate([jnp.where(own, repeated[k : k + 1], 0.0) for k in range(NFLUX)], axis=0)
        for copy in copies[:3]:
            copy.wait()
        t = jnp.tanh(held[...])
        sens = (held_adj[...] * (1.0 - t * t)).reshape(PLANES * ROWS, COLS)
        by_kind = jnp.dot(spread, sens, precision=lax.Precision.HIGHEST, preferred_element_type=f32)
        rows = []
        for q in range(4):
            rows.append(
                jnp.concatenate(
                    [by_kind[k * 4 : k * 4 + 4, q * 64 : q * 64 + 64] for k in range(NFLUX)], axis=1
                )
            )
        by_seg = jnp.concatenate(rows, axis=0)
        flux[0:16, :] = by_seg[:, 0:LANES]
        flux[16:32, :] = by_seg[:, LANES:]
        lane = iota((COLS, LANES), 1)
        pick = jnp.where(iota((COLS, LANES), 0) == (lane % 4) * 64 + 63 * (lane // 64), 1.0, 0.0).astype(bf16)
        ends = dot(jnp.concatenate(exact_parts(by_kind), axis=0).astype(bf16), pick)
        ends = ends[0:16] + ends[16:32] + ends[32:48]
        lane = iota((16, LANES), 1)
        mine = iota((16, LANES), 0) == (lane // 16 % 4) * 4 + lane // 4 % 4
        flux[32:33, :] = jnp.sum(jnp.where(mine, ends, 0.0), axis=0, keepdims=True)
        flux[33:40, :] = jnp.zeros((7, LANES), f32)


def adjoint_halo(from_north, from_south, f, l):
    high, low = from_north[PLANES + f], from_south[PLANES + f]
    if l:
        high, low = pltpu.roll(high, 4, 0), pltpu.roll(low, 4, 0)
    return jnp.where(iota((8, COLS), 0) < 4, high, low)


def strip_kernel(own_east, own_west, from_south, from_north, to_east, to_west):
    states = [jnp.concatenate([from_north[p], from_south[p]], axis=0) for p in range(PLANES)]
    states.append(jnp.concatenate([from_north[PLANES + FLD], from_south[PLANES + FLD]], axis=0))
    adjoints = [adjoint_halo(from_north, from_south, p // LEVB, p % LEVB) for p in range(PLANES)]
    for target, own in ((to_east, own_east), (to_west, own_west)):
        target[0:ROWS, :] = own[0]
        target[HALO_ROWS : HALO_ROWS + ROWS, :] = own[1]
    for start, planes in ((ROWS, states), (HALO_ROWS + ROWS, adjoints)):
        rows = slice(start, start + planes[0].shape[0])
        to_east[rows, :], to_west[rows, :] = packed_strips([x[:, 0:LANES] for x in planes], [x[:, LANES:] for x in planes])


def payload_kernel(flux, first, second, third, south, north, payload, block, sems):
    del south, north
    block[...] = flux[0:40, :] + (first[0:40, :] + second[0:40, :] + third[0:40, :])
    copies = [pltpu.make_async_copy(block, payload.at[tile], sems.at[tile]) for tile in range(TILES)]
    for copy in copies:
        copy.start()
    for copy in copies:
        copy.wait()


def to_adjoint_rows(x):
    row = iota((8, WIDE), 0)
    return jnp.concatenate([x[0:ROWS], jnp.where(row < 4, x[ROWS : ROWS + 8], x[ROWS + 8 :])], axis=0)


def pulled(mu, a, b, d):
    mixed, carried_e, carried_n = d * mu, a * mu, b * mu
    return (
        (1.0 - 4.0 * d) * mu
        + (east(mixed + carried_e) + west(mixed - carried_e))
        + (north(mixed + carried_n) + south(mixed - carried_n))
    )


def route_matrix(gathered, table, widen, high, low, code_t, prof_t, total, products, side_code):
    lat_me, lon_me = lax.axis_index("lat"), lax.axis_index("lon")

    def listed(at):
        parts = [gathered[pl.ds(33 + 2 * at + half, TILES, stride=40), :] for half in range(2)]
        return jnp.concatenate(parts, axis=1).astype(jnp.int32)

    def stacked(x):
        return jnp.concatenate([x[:, 0:LANES], x[:, LANES:]], axis=0)

    dest, row, profile = listed(0), listed(1), listed(2)
    dest_lat, dest_lon = jnp.right_shift(dest, 4), jnp.bitwise_and(dest, 15)
    row = row + ROWS * (dest_lat - lat_me)
    valid = jnp.logical_and(row >= -4, row < ROWS + 4)
    code = jnp.where(row < 0, row + ADJ_ROWS, row)
    is_east = dest_lon == (lon_me + 1) % 16
    is_west = dest_lon == (lon_me + 15) % 16
    own_code = jnp.where(jnp.logical_and(valid, dest_lon == lon_me), code.astype(f32), FAR)
    code_t[...] = stacked(own_code).T
    off = jnp.where(is_east, code, jnp.where(is_west, code + ADJ_ROWS, -1))
    side_code[...] = jnp.where(valid, off, -1).astype(f32)
    ends = jnp.concatenate(exact_parts(gathered[pl.ds(32, TILES, stride=40), :]), axis=0).astype(bf16)
    ends = dot(ends, widen[...])
    ends = ends[0:TILES] + ends[TILES : 2 * TILES] + ends[2 * TILES :]
    for c in range(4):
        weights = jnp.zeros((TILES, COLS), f32)
        for w in range(8):
            weights = jnp.where(profile == w, table[c, w], weights)
        prof_t[c] = stacked(weights).T
        for k in range(NFLUX):
            first, final = ends[:, k * COLS : (k + 1) * COLS], ends[:, (4 + k) * COLS : (5 + k) * COLS]
            at = (k * 4 + c) * TILES
            product = weights * jnp.where(is_east, first, final)
            products[0, at : at + TILES, :] = product[:, 0:LANES]
            products[1, at : at + TILES, :] = product[:, LANES:]
    own_matrix(code_t, prof_t, total, high, low)
    return side_sums(products, side_code)


def own_matrix(code_t, prof_t, total, high, low):
    rows = iota((ADJ_ROWS, LANES), 0).astype(f32)

    def build(seg, carry):
        sums = [jnp.zeros((ADJ_ROWS, LANES), f32) for _ in range(4)]
        for r in range(16):
            at = seg * 16 + r
            hit = code_t[pl.ds(at, 1), :] == rows
            for c in range(4):
                sums[c] = sums[c] + jnp.where(hit, prof_t[c, pl.ds(at, 1), :], 0.0)
        for c in range(4):
            total[seg, c] = sums[c]
        return carry

    lax.fori_loop(0, 8, build, 0)
    for seg in range(8):
        whole = total[seg].reshape(4 * ADJ_ROWS, LANES)
        head, tail = split(whole)
        high[:, seg * LANES : (seg + 1) * LANES] = head
        low[:, seg * LANES : (seg + 1) * LANES] = tail


def side_sums(products, side_code):
    bins = iota((2 * ADJ_ROWS, COLS), 0).astype(f32)

    def side(i, sums):
        for j in range(4):
            tile = i * 4 + j
            hit = jnp.where(side_code[pl.ds(tile, 1), :] == bins, 1.0, 0.0).astype(bf16)
            rows = pl.ds(tile, 16, stride=TILES)
            head, tail = split(jnp.concatenate([products[0, rows, :], products[1, rows, :]], axis=1))
            both = jnp.concatenate([head, tail], axis=0)
            sums = sums + lax.dot_general(hit, both, (((1,), (1,)), ((), ())), preferred_element_type=f32)
        return sums

    sums = lax.fori_loop(0, TILES // 4, side, jnp.zeros((2 * ADJ_ROWS, 32), f32))
    return sums[:, 0:16] + sums[:, 16:32]


def spread_tables():
    src, out = np.arange(512)[:, None], np.arange(512)[None, :]
    own = ((src // 64) % 2 == out // COLS) & (out % COLS == 4 * (src % 64) + src // 128)
    src, out = np.arange(LANES)[:, None], np.arange(8 * COLS)[None, :]
    seg = out % COLS // 16
    widen = (src // 16 == out // COLS) & (src % 16 == (seg // 4) * 4 + seg % 4)
    return own.astype(ml_dtypes.bfloat16), widen.astype(ml_dtypes.bfloat16)


def assemble_forcing(gathered, high, low, g_high, g_low, spread_own):
    for seg in range(8):
        for h in range(2):
            s = h * 8 + seg
            at = (s % 4) * 4 + s // 4
            for half in range(2):
                part = gathered[pl.ds(half * 16 + at, TILES, stride=40), :]
                head, tail = split(part)
                rows = slice(seg * LANES + h * 64, seg * LANES + h * 64 + 64)
                g_high[rows, half * LANES : (half + 1) * LANES] = head
                g_low[rows, half * LANES : (half + 1) * LANES] = tail
    coarse = dot(high[...], g_high[...]) + dot(high[...], g_low[...]) + dot(low[...], g_high[...])
    parts = []
    for half in range(2):
        cols = slice(half * LANES, (half + 1) * LANES)
        own = jnp.concatenate([coarse[c * ADJ_ROWS : (c + 1) * ADJ_ROWS, cols] for c in range(4)], axis=1)
        head = own.astype(bf16).astype(f32)
        parts += [head, own - head]
    return dot(jnp.concatenate(parts, axis=0).astype(bf16), spread_own[...])


def forward_steps(state, wet_all, diffusivity, speed_e, speed_n, grad_e, grad_n):
    for step in range(NSTEP):
        now, later = step % 2, (step + 1) % 2
        for l in range(LEVB):
            a = 0.5 * STEP_COEF * (SPEED_BASE + SPEED_GAIN * state[now, l])
            b = (0.5 * STEP_COEF * SPEED_GAIN) * state[now, LEVB + l]
            speed_e[step, l] = to_adjoint_rows(a)
            speed_n[step, l] = to_adjoint_rows(b)
            for f in range(FLD):
                d = diffusivity[f]
                q = state[now, f * LEVB + l]
                q_e, q_w, q_n, q_s = east(q), west(q), north(q), south(q)
                across, along = q_e - q_w, q_n - q_s
                half = -0.5 * STEP_COEF * SPEED_GAIN
                grad_e[step, f, l] = to_adjoint_rows(half * across)
                grad_n[step, f, l] = to_adjoint_rows(half * along)
                if step + 1 < NSTEP:
                    moved = (1.0 - 4.0 * d) * q + d * ((q_e + q_w) + (q_n + q_s)) - a * across - b * along
                    state[later, f * LEVB + l] = wet_all[...] * moved


def ocean_kernel(
    diffusivity_at,
    penetration_at,
    table_at,
    widen_at,
    spread_own_at,
    mask,
    checkpoint,
    adjoint_in,
    from_south,
    from_north,
    from_west,
    from_east,
    gathered,
    out,
    diffusivity,
    penetration,
    table,
    widen,
    spread_own,
    mask_own,
    state,
    lam,
    wet_all,
    wet,
    speed_e,
    speed_n,
    grad_e,
    grad_n,
    high,
    low,
    code_t,
    prof_t,
    total,
    products,
    side_code,
    g_high,
    g_low,
    done,
    sems,
):
    section = lax.axis_index("comp")
    pairs = [
        (diffusivity_at, diffusivity),
        (penetration_at, penetration),
        (table_at, table),
        (widen_at, widen),
        (spread_own_at, spread_own),
        (mask, mask_own),
    ]
    for plane in range(PLANES):
        f, l = plane // LEVB, plane % LEVB
        pairs.append((checkpoint.at[f, l], state.at[0, plane, 0:ROWS, 0:COLS]))
        pairs.append((adjoint_in.at[f, l], lam.at[f, l, 0:ROWS, 0:COLS]))
    copies = [pltpu.make_async_copy(source, target, sems.at[at]) for at, (source, target) in enumerate(pairs)]
    for copy in copies:
        copy.start()

    @pl.when(section == 3)
    def _():
        for copy in copies:
            copy.wait()
        for plane in range(PLANES):
            f, l = plane // LEVB, plane % LEVB
            t = jnp.tanh(state[0, plane, 0:ROWS, 0:COLS])
            done[f, l] = lam[f, l, 0:ROWS, 0:COLS] * (1.0 - t * t)

    @pl.when(section != 3)
    def _():
        for copy in copies[:5]:
            copy.wait()
        sides = route_matrix(gathered, table, widen, high, low, code_t, prof_t, total, products, side_code)
        own = assemble_forcing(gathered, high, low, g_high, g_low, spread_own)

        def edge(start, rows, plane):
            lane = iota((rows, LANES), 1)
            west_side, east_side = from_west[start : start + rows], from_east[start : start + rows]
            if plane:
                east_side = pltpu.roll(east_side, LANES - 8 * plane, 1)
            west_side = pltpu.roll(west_side, (120 - 8 * plane) % LANES, 1)
            return jnp.where(lane < 8, east_side, jnp.where(lane >= 120, west_side, 0.0))

        for f in range(FLD):
            for l in range(LEVB):
                plane = f * LEVB + l
                state[0, plane, ROWS : ROWS + 8, 0:COLS] = from_north[plane]
                state[0, plane, ROWS + 8 :, 0:COLS] = from_south[plane]
                state[0, plane, :, COLS:] = edge(0, HALO_ROWS, plane)
                lam[f, l, ROWS:, 0:COLS] = adjoint_halo(from_north, from_south, f, l)
                lam[f, l, :, COLS:] = edge(HALO_ROWS, ADJ_ROWS, plane)
        at = PLANES + FLD
        for copy in copies[5:]:
            copy.wait()
        wet_all[0:ROWS, 0:COLS] = mask_own[...].astype(f32)
        wet_all[ROWS : ROWS + 8, 0:COLS] = from_north[at]
        wet_all[ROWS + 8 :, 0:COLS] = from_south[at]
        wet_all[:, COLS:] = edge(0, HALO_ROWS, PLANES)
        wet[...] = to_adjoint_rows(wet_all[...])
        lane = iota((ADJ_ROWS, LANES), 1)
        sides = jnp.concatenate([sides, jnp.zeros((2 * ADJ_ROWS, LANES - 16), f32)], axis=1)
        w = wet[...]
        band = lax.axis_index("comp")
        for k in range(NFLUX):
            at, sub = (k // 2) * 2 * ADJ_ROWS, k % 2
            own_k = own[:, sub * COLS : (sub + 1) * COLS]
            own_k = own_k[at : at + ADJ_ROWS] + own_k[at + ADJ_ROWS : at + 2 * ADJ_ROWS]
            first, final = sides[0:ADJ_ROWS], sides[ADJ_ROWS:]
            if k:
                first = pltpu.roll(first, LANES - 4 * k, 1)
            final = pltpu.roll(final, LANES - 4 * k - 4, 1)
            side_k = jnp.where(lane < 4, first, jnp.where(lane >= LANES - 4, final, 0.0))
            forcing = w * jnp.concatenate([own_k, side_k], axis=1)
            for l in range(LEVB):
                lam[k, l] = lam[k, l] + penetration[band * LEVB + l] * forcing

        forward_steps(state, wet_all, diffusivity, speed_e, speed_n, grad_e, grad_n)

        def back(i, carry):
            step = NSTEP - 1 - i
            for l in range(LEVB):
                a, b, w = speed_e[step, l], speed_n[step, l], wet[...]
                sum_e, sum_n = 0.0, 0.0
                for f in (2, 3, 4, 5, 1, 0):
                    mu = w * lam[f, l]
                    sum_e = sum_e + mu * grad_e[step, f, l]
                    sum_n = sum_n + mu * grad_n[step, f, l]
                    lam[f, l] = pulled(mu, a, b, diffusivity[f])
                lam[0, l] = lam[0, l] + sum_e
                lam[1, l] = lam[1, l] + sum_n
            return carry

        lax.fori_loop(0, NSTEP, back, 0)
        for f in range(FLD):
            for l in range(LEVB):
                done[f, l] = lam[f, l, 0:ROWS, 0:COLS]

    copy = pltpu.make_async_copy(done, out, sems.at[0])
    copy.start()
    copy.wait()


def shards(
    checkpoint,
    adjoint_in,
    land_mask,
    diffusivity,
    penetration,
    column_weight,
    routes,
    dest_row,
    weight_id,
    regrid_table,
):
    state, adj = checkpoint[0], adjoint_in[0]
    state_at, adj_at, mask_at = hbm(state), hbm(adj), hbm(land_mask)
    any_place = pl.BlockSpec(memory_space=pl.ANY)
    held = VM((FLD, LEVB, ROWS, COLS), f32)
    edge = shape_of((PLANES + FLD + 1, 8, COLS))
    own_strip = shape_of((2, ROWS, LANES))
    pairs = (2, LANES)
    small = pltpu.CompilerParams(vmem_limit_bytes=2 << 20)
    flux, to_north, to_south, own_east, own_west = pl.pallas_call(
        flux_kernel,
        out_shape=(shape_of((40, LANES)), edge, edge, own_strip, own_strip),
        in_specs=[in_hbm()] * 7,
        out_specs=(vmem(),) * 5,
        scratch_shapes=[
            held,
            held,
            VM((ROWS, COLS), jnp.int32),
            VM((NFLUX, FLD * 32), f32),
            VM((8, LANES), jnp.int32),
            pltpu.SemaphoreType.DMA((7,)),
        ],
        compiler_params=pltpu.CompilerParams(vmem_limit_bytes=12 << 20),
        name="flux",
    )(
        state_at,
        adj_at,
        mask_at,
        *[hbm(x) for x in (column_weight, routes.reshape(pairs), dest_row.reshape(pairs), weight_id.reshape(pairs))],
    )
    sent = [lax.ppermute(flux, "comp", [(3, band)]) for band in range(3)]
    rows_up = [(c * 4 + i, c * 4 + i + 1) for c in range(3) for i in range(3)]
    from_south = lax.ppermute(to_north, ("comp", "lat"), rows_up)
    from_north = lax.ppermute(to_south, ("comp", "lat"), [(b, a) for a, b in rows_up])

    payload = pl.pallas_call(
        payload_kernel,
        out_shape=pltpu.HBM((TILES, 40, LANES), f32),
        in_specs=[vmem()] * 4 + [any_place] * 2,
        out_specs=in_hbm(),
        scratch_shapes=[VM((40, LANES), f32), pltpu.SemaphoreType.DMA((TILES,))],
        compiler_params=small,
        name="payload",
    )(flux, *sent, from_south, from_north)

    strip = shape_of((HALO_ROWS + ADJ_ROWS, LANES))
    to_east, to_west = pl.pallas_call(
        strip_kernel,
        out_shape=(strip, strip),
        in_specs=[vmem()] * 4,
        out_specs=(vmem(),) * 2,
        compiler_params=pltpu.CompilerParams(vmem_limit_bytes=8 << 20),
        name="strips",
    )(own_east, own_west, from_south, from_north)
    cols_up = [(c * 16 + i, c * 16 + (i + 1) % 16) for c in range(3) for i in range(16)]
    from_west = lax.ppermute(to_east, ("comp", "lon"), cols_up)
    from_east = lax.ppermute(to_west, ("comp", "lon"), [(b, a) for a, b in cols_up])

    gathered = lax.all_to_all(payload, ("lat", "lon"), split_axis=0, concat_axis=0, tiled=True)
    gathered = gathered.reshape(TILES * 40, LANES)

    spread_own, widen = spread_tables()
    wide = (ADJ_ROWS, WIDE)
    result = pl.pallas_call(
        ocean_kernel,
        out_shape=pltpu.HBM((FLD, LEVB, ROWS, COLS), f32),
        in_specs=[in_hbm()] * 8 + [vmem()] * 5,
        out_specs=in_hbm(),
        scratch_shapes=[
            SM((FLD,), f32),
            SM((FLD,), f32),
            SM((4, 8), f32),
            VM((LANES, 8 * COLS), bf16),
            VM((512, 512), bf16),
            VM((ROWS, COLS), jnp.int32),
            VM((2, PLANES, HALO_ROWS, WIDE), f32),
            VM((FLD, LEVB) + wide, f32),
            VM((HALO_ROWS, WIDE), f32),
            VM(wide, f32),
            VM((NSTEP, LEVB) + wide, f32),
            VM((NSTEP, LEVB) + wide, f32),
            VM((NSTEP, FLD, LEVB) + wide, f32),
            VM((NSTEP, FLD, LEVB) + wide, f32),
            VM((4 * ADJ_ROWS, 1024), bf16),
            VM((4 * ADJ_ROWS, 1024), bf16),
            VM((LANES, LANES), f32),
            VM((4, LANES, LANES), f32),
            VM((8, 4, ADJ_ROWS, LANES), f32),
            VM((2, 16 * TILES, LANES), f32),
            VM((TILES, COLS), f32),
            VM((1024, COLS), bf16),
            VM((1024, COLS), bf16),
            held,
            pltpu.SemaphoreType.DMA((6 + 2 * PLANES,)),
        ],
        compiler_params=pltpu.CompilerParams(vmem_limit_bytes=48 << 20),
        name="ocean",
    )(
        *[hbm(x) for x in (diffusivity, penetration, regrid_table.T, widen, spread_own)],
        mask_at,
        state_at,
        adj_at,
        from_south,
        from_north,
        from_west,
        from_east,
        gathered,
    )
    return result[None]


def solution(mesh):
    in_specs = (
        P("comp", None, None, "lat", "lon"),
        P("comp", None, None, "lat", "lon"),
        P("lat", "lon"),
        P(),
        P(),
        P(),
        P(("lat", "lon"), None),
        P(("lat", "lon")),
        P(("lat", "lon")),
        P(),
    )
    out_specs = P("comp", None, None, "lat", "lon")
    return jax.shard_map(shards, mesh=mesh, in_specs=in_specs, out_specs=out_specs, check_vma=False)
```
